512 devices in a mesh: kern: 64 (over y, z), walk: 8 (over x, core).
Axes of the slice: x: 4, y: 8, z: 8, core: 2. Of those that a mesh axis runs over, the one named last changes fastest.
Arguments:
- walkers: float32 [8, 8192], P(None, 'walk'), may hold values from -5 to 5
- centers: float32 [8, 131072], P(None, 'kern'), may hold values from -5 to 5
- sigmas: float32 [8, 131072], P(None, 'kern'), may hold values from 0.6 to 1.5
- heights: float32 [131072], P('kern'), may hold values from 0.2 to 2
- kernel_live: int32 [64], P('kern'), may hold values from 512 to 2048, as said below
- merge_target: int32 [8192], P('walk'), may hold values from 0 to 131071, as said below
- new_sigma: float32 [8], replicated, may hold values from 0.2 to 0.6
- norm_old: float32 [1], replicated, may hold values from 0.003 to 0.03
Outputs:
- bias: float32 [8192], P('walk')
- force: float32 [8, 8192], P(None, 'walk')
- new_heights: float32 [131072], P('kern')
- new_centers: float32 [8, 131072], P(None, 'kern')
- new_sigmas: float32 [8, 131072], P(None, 'kern')
- log_norm: float32 [1], replicated
The draws below stay inside these ranges and needn't reach their ends.
Inputs may be any that keep to these rules, and one draw needn't show every extreme that they name: `kernel_live`: slots from this number up are empty; some shard is full in every draw. `merge_target`: each entry is shard * 2048 + slot with slot below that shard's kernel_live; among the 1024 walkers of one index of walk at most 32 target one shard, every shard is targeted, and some shard receives exactly 32 in every block.
All inputs are finite; a program needn't handle non-finite values.
Results may differ from the reference program's by a relative error of at most 0.0003.
Values sent between devices are 32-bit elements; how exact they have to be, the bound alone decides.
No kernel may reach another device: no remote copies, remote signals or barrier semaphores. Data moves between devices by JAX's collectives and lax.ppermute only.
A program may use at most 64 MiB of HBM per device.

```python
import math
import jax
import jax.numpy as jnp
from jax import lax

DIMS = 8
KS = 2048
WB = 1024
KERNELS = 131072
WALKERS = 8192
N_KERN = 64
N_WALK = 8


def live_table(key):
    first, second = jax.random.split(jax.random.fold_in(key, 11))
    live_count = jax.random.randint(first, (N_KERN,), KS // 4, KS + 1)
    fullest = jax.random.randint(second, (), 0, N_KERN)
    return jnp.where(jnp.arange(N_KERN) == fullest, KS, live_count).astype(jnp.int32)


def draw_kernel_live(key, part):
    return live_table(key)


def block_shards(block_key):
    capacity = 2 * WB // N_KERN
    key_busy, key_pick, key_order = jax.random.split(block_key, 3)
    busiest = jax.random.randint(key_busy, (), 0, N_KERN)
    others = (busiest + 1 + jnp.arange(N_KERN - 1)) % N_KERN
    units = (N_KERN - 1) * (capacity - 1)
    extra = WB - capacity - (N_KERN - 1)
    picked = jax.random.permutation(key_pick, units)[:extra]
    listed = jnp.concatenate([jnp.full((capacity,), busiest), others, others[picked // (capacity - 1)]])
    return jax.random.permutation(key_order, listed)


def draw_merge_target(key, part):
    live_count = live_table(key)
    block_keys = jax.random.split(jax.random.fold_in(key, 31), N_WALK)
    shards = jax.vmap(block_shards)(block_keys).reshape(-1)
    raw_slot = jax.random.randint(jax.random.fold_in(key, 47), (WALKERS,), 0, 1 << 30)
    slot = raw_slot % live_count[shards]
    return (shards * KS + slot).astype(jnp.int32)


def levels(rng, dims, cuts, smallest, top_value):
    def one(axis_at, shards_of):
        steps = jax.random.uniform(jax.random.fold_in(jax.random.fold_in(rng, 6), axis_at), (shards_of,), jnp.float32, smallest / len(cuts), top_value / len(cuts))
        return jnp.repeat(jnp.exp(steps), dims[axis_at] // shards_of).reshape((-1,) + (1,) * (len(dims) - axis_at - 1))

    gain = one(*cuts[0])
    for cut in cuts[1:]:
        gain = gain * one(*cut)
    return gain


def noise(own_key, shape, spread, bound, cuts=(), kind=jnp.bfloat16):
    loudness = levels(own_key, shape, cuts, -0.22, 0.18) if cuts else 1.0
    values = jax.random.normal(own_key, shape, jnp.float32) * spread * loudness
    return jnp.minimum(jnp.maximum(values, -bound), bound).astype(kind)


def setup_inputs(seed: int = 0) -> dict:
    key_of = jax.random.split(jax.random.key(seed), 9)
    return {
        "walkers": noise(key_of[0], (DIMS, WALKERS), 1.0, 5.0, ((1, 8),), jnp.float32),
        "centers": noise(key_of[1], (DIMS, KERNELS), 1.0, 5.0, ((1, 64),), jnp.float32),
        "sigmas": jnp.clip(jnp.exp(math.log(1.5) - 0.9162907 * jax.random.uniform(key_of[2], (DIMS, KERNELS), jnp.float32) ** levels(key_of[2], (DIMS, KERNELS), ((1, 64),), -0.2, 0.2)), 0.6, 1.5),
        "heights": jnp.clip(jnp.exp(math.log(2.0) - 2.3025851 * jax.random.uniform(key_of[3], (KERNELS,), jnp.float32) ** levels(key_of[3], (KERNELS,), ((0, 64),), -0.2, 0.2)), 0.2, 2.0),
        "kernel_live": draw_kernel_live(jax.random.fold_in(key_of[8], 71), 0),
        "merge_target": draw_merge_target(jax.random.fold_in(key_of[8], 71), 0),
        "new_sigma": jnp.clip(jnp.exp(jax.random.uniform(key_of[6], (DIMS,), jnp.float32, math.log(0.2), math.log(0.6))), 0.2, 0.6),
        "norm_old": jnp.clip(jnp.exp(jax.random.uniform(key_of[7], (1,), jnp.float32, math.log(0.003), math.log(0.03))), 0.003, 0.03),
    }


PREFACTOR = 0.9
EPSILON = 0.01
RATE = 0.25

def reference(walkers, centers, sigmas, heights, kernel_live, merge_target, new_sigma, norm_old):
    inverse_var = 1.0 / (sigmas * sigmas)
    slot_of = jnp.arange(KERNELS, dtype=jnp.int32) % KS
    alive = (slot_of < jnp.repeat(kernel_live, KS)).astype(jnp.float32)
    kernel_feat = jnp.concatenate([-0.5 * inverse_var, centers * inverse_var, (jnp.log(heights) - 0.5 * lax.optimization_barrier(jnp.sum(centers * centers * inverse_var, 0)))[None]], 0)
    kernel_mom = jnp.concatenate([alive[None], inverse_var * alive, centers * inverse_var * alive], 0)
    walker_feat = jnp.concatenate([walkers * walkers, walkers, jnp.ones((1, WALKERS), jnp.float32)], 0)
    block_len = 1024 if KERNELS % 1024 == 0 else KS
    block_count = KERNELS // block_len

    def step(running, block_index):
        start = (block_index * block_len).astype(jnp.int32)
        feat = lax.dynamic_slice_in_dim(kernel_feat, start, block_len, 1)
        moms = lax.dynamic_slice_in_dim(kernel_mom, start, block_len, 1)
        expo = lax.dot_general(feat, walker_feat, (((0,), (0,)), ((), ())), precision=lax.Precision.HIGHEST)
        return (running + jnp.dot(moms, jnp.exp(expo), precision=lax.Precision.HIGHEST), None)
    moments, _ = lax.scan(step, jnp.zeros((17, WALKERS), jnp.float32), jnp.arange(block_count, dtype=jnp.int32))
    live_total = jnp.sum(kernel_live).astype(jnp.float32)
    density = moments[0] / live_total
    grad = (-walkers * moments[1:9] + moments[9:17]) / live_total
    norm_value = norm_old[0]
    ratio = density / norm_value + EPSILON
    bias = PREFACTOR * jnp.log(ratio)
    force = -PREFACTOR * grad / (norm_value * ratio)
    weight = jnp.exp(bias)
    log_norm = jnp.log((1.0 - RATE) * norm_old + RATE * jnp.sum(density) / WALKERS)
    target_center = centers[:, merge_target]
    offset = walkers - target_center
    feat = jnp.concatenate([weight[None], weight * offset, weight * (offset * offset + (new_sigma * new_sigma)[:, None])], 0)
    merged_sums = jax.ops.segment_sum(feat.T, merge_target, KERNELS).T
    new_heights = heights + merged_sums[0]
    delta = merged_sums[1:9] / new_heights
    new_centers = centers + delta
    new_sigmas = jnp.sqrt((heights * sigmas * sigmas + merged_sums[9:17]) / new_heights - delta * delta)
    return (bias, force, new_heights, new_centers, new_sigmas, log_norm)
```

```python
import functools
import jax
import jax.numpy as jnp
from jax import lax
from jax.experimental import pallas as pl
from jax.experimental.pallas import tpu as pltpu
from jax.sharding import PartitionSpec as P

PREFACTOR = 0.9
EPSILON = 0.01
RATE = 0.25
LOG2E = 1.4426950408889634
F32 = jnp.float32
BF16 = jnp.bfloat16
NT = (((1,), (1,)), ((), ()))
VMEM = pl.BlockSpec(memory_space=pltpu.VMEM)
SMEM = pl.BlockSpec(memory_space=pltpu.SMEM)


def split3(x):
    hi = x.astype(BF16).astype(F32)
    rest = x - hi
    mid = rest.astype(BF16).astype(F32)
    return (hi, mid, rest - mid)


def as_row(x):
    return jnp.concatenate([x[r : r + 1, :] for r in range(x.shape[0])], axis=1)


def stacked(x):
    return jnp.concatenate([x[:, 128 * c : 128 * c + 128] for c in range(x.shape[1] // 128)], axis=0)


def moments_kernel(
    bw, bk, nk, walkers, centers, sigmas, heights, live, target, sums_out, rows_out,
    lhs, rhs, mom, own,
):
    kernels = centers.shape[1]
    count = walkers.shape[1]
    shard = lax.axis_index("kern")
    s = sigmas[...]
    c = centers[...]
    inv = 1.0 / (s * s)
    ca = c * inv
    const = as_row(jnp.log(heights[...])) - 0.5 * jnp.sum(c * ca, axis=0, keepdims=True)
    kf = jnp.concatenate([(-0.5 * LOG2E) * inv, LOG2E * ca], axis=0)
    k1, k2, k3 = split3(kf)
    c1, c2, c3 = split3(const * LOG2E)
    pad = jnp.zeros((13, kernels), F32)
    rhs[...] = jnp.concatenate(
        [k1, k2, k3, k1, k2, k1, c1, c2, c3, pad, jnp.zeros((16, kernels), F32)], axis=0
    ).astype(BF16)
    alive = (lax.broadcasted_iota(jnp.int32, (1, kernels), 1) < live[0]).astype(F32)
    km = jnp.concatenate([inv, ca], axis=0) * alive
    m1, m2, _ = split3(km)
    mom[...] = jnp.concatenate([m1, m2, alive, jnp.zeros((15, kernels), F32)], axis=0).astype(BF16)
    w = walkers[...]
    wf = jnp.concatenate([w * w, w], axis=0)
    w1, w2, w3 = split3(wf)
    ones = (lax.broadcasted_iota(jnp.int32, (16, count), 0) < 3).astype(F32)
    feats = jnp.concatenate([w1, w1, w1, w2, w2, w3, ones, jnp.zeros((16, count), F32)], axis=0)
    lhs[...] = jnp.concatenate(
        [jnp.transpose(feats[:, 128 * i : 128 * i + 128]) for i in range(count // 128)], axis=0
    ).astype(BF16)
    parts = []
    for i in range(count // bw):
        left = lhs[bw * i : bw * i + bw, :]
        total = jnp.zeros((bw, 48), F32)
        for j in range(kernels // bk):
            expo = jnp.dot(left, rhs[:, bk * j : bk * j + bk], preferred_element_type=F32)
            e = jnp.exp2(expo)
            e1 = e.astype(BF16)
            e2 = (e - e1.astype(F32)).astype(BF16)
            m = mom[:, bk * j : bk * j + bk]
            total += lax.dot_general(e1, m, NT, preferred_element_type=F32)
            total += lax.dot_general(e2, m, NT, preferred_element_type=F32)
        for b in range(bw // 128):
            wide = jnp.concatenate([total[128 * b : 128 * b + 128], jnp.zeros((128, 80), F32)], axis=1)
            parts.append(jnp.transpose(wide)[0:48])
    summed = jnp.concatenate(parts, axis=1)
    inv_sum = summed[0:8] + summed[16:24]
    ca_sum = summed[8:16] + summed[24:32]
    density = summed[32:33]
    t = as_row(target[...])
    shard_of = t // kernels
    slot_of = t - shard_of * kernels
    member = (lax.broadcasted_iota(jnp.int32, (nk, count), 0) == shard_of).astype(F32)
    member16 = member.astype(BF16)
    ra = lax.broadcasted_iota(jnp.int32, (128, 256), 0)
    rb = lax.broadcasted_iota(jnp.int32, (128, 256), 1)
    before = ((ra < rb) | (rb >= 128)).astype(BF16)
    counts = jnp.dot(
        jnp.concatenate([member16[:, 128 * i : 128 * i + 128] for i in range(count // 128)], axis=0),
        before,
        preferred_element_type=F32,
    )
    base = jnp.zeros((nk, 128), F32)
    ranks = []
    for i in range(count // 128):
        here = counts[nk * i : nk * i + nk]
        ranks.append(
            jnp.sum(member[:, 128 * i : 128 * i + 128] * (base + here[:, 0:128]), axis=0, keepdims=True)
        )
        base = base + here[:, 128:256]
    rank = jnp.concatenate(ranks, axis=1).astype(jnp.int32)
    placed = (lax.broadcasted_iota(jnp.int32, (128, count), 0) == rank).astype(F32)
    d1, d2, d3 = split3(density)
    compact = jnp.zeros((nk, 128), F32)
    for d in (d1, d2, d3):
        compact += lax.dot_general(member16, (placed * d).astype(BF16), NT, preferred_element_type=F32)
    lane = lax.broadcasted_iota(jnp.int32, (nk, 128), 1)
    compact = jnp.where(lane == 32, jnp.sum(density), compact)
    compact = jnp.where(lane == 33, live[0].astype(F32), compact)
    both = jnp.transpose(jnp.concatenate([stacked(inv_sum), stacked(ca_sum)], axis=0))
    sums_out[:, 0, :] = both[0:64]
    sums_out[:, 1, :] = both[64:128]
    dens = stacked(jnp.broadcast_to(density, (8, count)))
    turned = jnp.transpose(jnp.concatenate([dens, stacked(w)], axis=0))
    sums_out[:, 2, :] = jnp.concatenate([turned[0:64, 0:64], turned[64:128, 0:64]], axis=1)
    sums_out[:, 3, :] = compact
    own[...] = jnp.concatenate([turned[0:64, 64:128], turned[64:128, 64:128]], axis=1)
    mine = (placed * (shard_of == shard).astype(F32)).astype(BF16)
    x1, x2, x3 = split3(jnp.concatenate([w, jnp.broadcast_to((slot_of + 1).astype(F32), (8, count))], axis=0))
    rows = jnp.zeros((16, 128), F32)
    for x in (x1, x2, x3):
        rows += lax.dot_general(x.astype(BF16), mine, NT, preferred_element_type=F32)
    rows_out[0:16, :] = rows
    rows_out[16:24, :] = jnp.broadcast_to(own[pl.ds(shard, 1), :], (8, 128))


def results_kernel(got, rows, norm, results_out, merge_out):
    block = lax.axis_index("walk")
    total = jnp.sum(got[...], axis=0)
    live_total = total[3:4, 33:34]
    norm_value = norm[0]
    coords = rows[16:17, :]
    lane = lax.broadcasted_iota(jnp.int32, (1, 128), 1)
    first = lane < 64
    inv_sum = jnp.where(first, total[0:1], pltpu.roll(total[1:2], 64, 1))
    ca_sum = jnp.where(first, pltpu.roll(total[0:1], 64, 1), total[1:2])
    both = jnp.concatenate([total[2:3], total[3:4]], axis=0) / live_total
    ratio = both / norm_value + EPSILON
    bias = PREFACTOR * jnp.log(ratio)
    weight = jnp.exp(bias[1:2])
    grad = (-coords * inv_sum + ca_sum) / live_total
    force = -PREFACTOR * grad / (norm_value * ratio[0:1])
    out = jnp.concatenate([force, bias[0:1]], axis=0)
    results_out[...] = jnp.broadcast_to(out[None], results_out.shape)
    shift = 32 * (block % 4)
    weight = jnp.where(lane < 32, weight, 0.0)
    share = jnp.where(lane == 32, both[1:2], 0.0)
    tail = jnp.concatenate(
        [rows[8:9, :], weight, jnp.broadcast_to(jnp.sum(share, axis=1, keepdims=True), (1, 128)),
         jnp.zeros((5, 128), F32)], axis=0)
    packed = jnp.concatenate([rows[0:8, :], tail], axis=0)
    packed = pltpu.roll(packed, shift, 1)
    merge_out[...] = jnp.broadcast_to(packed[None], merge_out.shape)


def merge_kernel(walker_count, got, centers, sigmas, heights, sigma_new, norm,
                 heights_out, centers_out, sigmas_out, norm_out):
    kernels = centers.shape[1]
    first = got[0] + got[1] + got[2] + got[3]
    second = got[4] + got[5] + got[6] + got[7]
    cand = jnp.concatenate([first, second], axis=1)
    x = cand[0:8]
    slot = cand[8:9].astype(jnp.int32) - 1
    weight = cand[9:10]
    density_sum = first[10:11, 0:1] + second[10:11, 0:1]
    placing = (lax.broadcasted_iota(jnp.int32, (kernels, 256), 0) == slot).astype(BF16)
    c = centers[...]
    at = jnp.zeros((8, 256), F32)
    for part in split3(c):
        at += jnp.dot(part.astype(BF16), placing, preferred_element_type=F32)
    offset = x - at
    sub = lax.broadcasted_iota(jnp.int32, (8, 1), 0)
    sn = jnp.zeros((8, 1), F32)
    for d in range(8):
        sn = jnp.where(sub == d, sigma_new[d], sn)
    feat = jnp.concatenate(
        [jnp.broadcast_to(weight, (8, 256)), weight * offset, weight * (offset * offset + sn * sn)], axis=0
    )
    sums = jnp.zeros((24, kernels), F32)
    for part in split3(feat):
        sums += lax.dot_general(part.astype(BF16), placing, NT, preferred_element_type=F32)
    h = as_row(heights[...])
    new_h = h + sums[0:1]
    delta = sums[8:16] / new_h
    s = sigmas[...]
    centers_out[...] = c + delta
    sigmas_out[...] = jnp.sqrt((h * s * s + sums[16:24]) / new_h - delta * delta)
    heights_out[...] = jnp.concatenate([new_h[:, 128 * r : 128 * r + 128] for r in range(kernels // 128)], axis=0)
    norm_out[...] = jnp.log((1.0 - RATE) * norm[0] + RATE * density_sum / walker_count)


def spread_kernel(got, bias_out, force_out):
    for row, out in ((0, force_out), (1, None)):
        v = got[:, row, :]
        v = jnp.concatenate([v[:, 0:64], v[:, 64:128]], axis=0)
        v = jnp.concatenate([v, jnp.zeros((128, 64), F32)], axis=1)
        v = jnp.transpose(v)
        for g in range(8):
            if row == 0:
                out[:, 128 * g : 128 * g + 128] = v[8 * g : 8 * g + 8]
            else:
                bias_out[g : g + 1, :] = v[8 * g : 8 * g + 1]


def call(kernel, outs, specs, scratch=(), cost=None):
    many = isinstance(outs, (list, tuple))
    return pl.pallas_call(
        kernel,
        out_shape=outs,
        in_specs=specs,
        out_specs=[VMEM] * len(outs) if many else VMEM,
        scratch_shapes=list(scratch),
        cost_estimate=cost,
        compiler_params=pltpu.CompilerParams(vmem_limit_bytes=40 * 2**20),
    )


def shape(*dims):
    return jax.ShapeDtypeStruct(dims, F32)


def per_device(walkers, centers, sigmas, heights, kernel_live, merge_target, new_sigma, norm_old):
    nk = lax.axis_size("kern")
    nw = lax.axis_size("walk")
    kernels = centers.shape[1]
    count = walkers.shape[1]
    heights2 = heights.reshape(-1, 128)
    sums, rows = call(
        functools.partial(moments_kernel, BW, BK, nk),
        [shape(nk, 4, 128), shape(24, 128)],
        [VMEM, VMEM, VMEM, VMEM, SMEM, VMEM],
        [
            pltpu.VMEM((count, 128), BF16),
            pltpu.VMEM((128, kernels), BF16),
            pltpu.VMEM((48, kernels), BF16),
            pltpu.VMEM((nk, 128), F32),
        ],
    )(walkers, centers, sigmas, heights2, kernel_live, merge_target.reshape(-1, 128))
    sums = lax.all_to_all(sums, "kern", 0, 0, tiled=True)
    results, packed = call(
        results_kernel,
        [shape(nk, 2, 128), shape(nw, 16, 128)],
        [VMEM, VMEM, SMEM],
    )(sums, rows, norm_old)
    results = lax.all_to_all(results, "kern", 0, 0, tiled=True)
    packed = lax.all_to_all(packed, "walk", 0, 0, tiled=True)
    new_heights, new_centers, new_sigmas, log_norm = call(
        functools.partial(merge_kernel, count * nw),
        [shape(*heights2.shape), shape(*centers.shape), shape(*centers.shape), shape(1, 1)],
        [VMEM, VMEM, VMEM, VMEM, SMEM, SMEM],
        cost=pl.CostEstimate(flops=10**9, bytes_accessed=10**6, transcendentals=0),
    )(packed, centers, sigmas, heights2, new_sigma, norm_old)
    bias, force = call(spread_kernel, [shape(count // 128, 128), shape(8, count)], [VMEM])(results)
    return (
        bias.reshape(-1), force, new_heights.reshape(-1), new_centers, new_sigmas, log_norm.reshape(-1)
    )


BW = 256
BK = 256


def solution(mesh):
    in_specs = (
        P(None, "walk"),
        P(None, "kern"),
        P(None, "kern"),
        P("kern"),
        P("kern"),
        P("walk"),
        P(),
        P(),
    )
    out_specs = (P("walk"), P(None, "walk"), P("kern"), P(None, "kern"), P(None, "kern"), P())
    return jax.shard_map(
        per_device, mesh=mesh, in_specs=in_specs, out_specs=out_specs, check_vma=False
    )
```

```python
import functools
import jax
import jax.numpy as jnp
from jax import lax
from jax.experimental import pallas as pl
from jax.experimental.pallas import tpu as pltpu
from jax.sharding import Mesh
from jax.sharding import PartitionSpec as P

WALK = ("wx", "wc")
PREFACTOR = 0.9
EPSILON = 0.01
RATE = 0.25
LOG2E = 1.4426950408889634
F32 = jnp.float32
BF16 = jnp.bfloat16
NT = (((1,), (1,)), ((), ()))
VMEM = pl.BlockSpec(memory_space=pltpu.VMEM)
HBM = pl.BlockSpec(memory_space=pltpu.HBM)
SMEM = pl.BlockSpec(memory_space=pltpu.SMEM)


def split3(x):
    hi = x.astype(BF16).astype(F32)
    rest = x - hi
    mid = rest.astype(BF16).astype(F32)
    return (hi, mid, rest - mid)


def as_row(x):
    return jnp.concatenate([x[r : r + 1, :] for r in range(x.shape[0])], axis=1)


def stacked(x):
    return jnp.concatenate([x[:, 128 * c : 128 * c + 128] for c in range(x.shape[1] // 128)], axis=0)


def moments_kernel(
    bw, bk, nk, walkers_in, centers_in, sigmas_in, heights_in, live, target_in, sums_out, rows_out,
    lhs, rhs, mom, own, walkers, centers, sigmas, heights, target, sems,
):
    copies = [
        pltpu.make_async_copy(src, dst, sems.at[n])
        for n, (src, dst) in enumerate((
            (sigmas_in, sigmas), (centers_in, centers), (heights_in, heights), (walkers_in, walkers),
            (target_in, target),
        ))
    ]
    for copy in copies:
        copy.start()
    for copy in copies:
        copy.wait()
    kernels = centers.shape[1]
    count = walkers.shape[1]
    shard = lax.axis_index("kern")
    s = sigmas[...]
    c = centers[...]
    inv = 1.0 / (s * s)
    ca = c * inv
    const = as_row(jnp.log(heights[...])) - 0.5 * jnp.sum(c * ca, axis=0, keepdims=True)
    kf = jnp.concatenate([(-0.5 * LOG2E) * inv, LOG2E * ca], axis=0)
    k1, k2, k3 = split3(kf)
    c1, c2, c3 = split3(const * LOG2E)
    pad = jnp.zeros((13, kernels), F32)
    rhs[...] = jnp.concatenate(
        [k1, k2, k3, k1, k2, k1, c1, c2, c3, pad, jnp.zeros((16, kernels), F32)], axis=0
    ).astype(BF16)
    alive = (lax.broadcasted_iota(jnp.int32, (1, kernels), 1) < live[0]).astype(F32)
    km = jnp.concatenate([inv, ca], axis=0) * alive
    m1, m2, _ = split3(km)
    mom[...] = jnp.concatenate([m1, m2, alive, jnp.zeros((15, kernels), F32)], axis=0).astype(BF16)
    w = walkers[...]
    wf = jnp.concatenate([w * w, w], axis=0)
    w1, w2, w3 = split3(wf)
    ones = (lax.broadcasted_iota(jnp.int32, (16, count), 0) < 3).astype(F32)
    feats = jnp.concatenate([w1, w1, w1, w2, w2, w3, ones, jnp.zeros((16, count), F32)], axis=0)
    lhs[...] = jnp.concatenate(
        [jnp.transpose(feats[:, 128 * i : 128 * i + 128]) for i in range(count // 128)], axis=0
    ).astype(BF16)
    parts = []
    for i in range(count // bw):
        left = lhs[bw * i : bw * i + bw, :]
        total = jnp.zeros((bw, 48), F32)
        for j in range(kernels // bk):
            expo = jnp.dot(left, rhs[:, bk * j : bk * j + bk], preferred_element_type=F32)
            e = jnp.exp2(expo)
            e1 = e.astype(BF16)
            e2 = (e - e1.astype(F32)).astype(BF16)
            m = mom[:, bk * j : bk * j + bk]
            total += lax.dot_general(e1, m, NT, preferred_element_type=F32)
            total += lax.dot_general(e2, m, NT, preferred_element_type=F32)
        for b in range(bw // 128):
            wide = jnp.concatenate([total[128 * b : 128 * b + 128], jnp.zeros((128, 80), F32)], axis=1)
            parts.append(jnp.transpose(wide)[0:48])
    summed = jnp.concatenate(parts, axis=1)
    inv_sum = summed[0:8] + summed[16:24]
    ca_sum = summed[8:16] + summed[24:32]
    density = summed[32:33]
    t = as_row(target[...])
    shard_of = t // kernels
    slot_of = t - shard_of * kernels
    member = (lax.broadcasted_iota(jnp.int32, (nk, count), 0) == shard_of).astype(F32)
    member16 = member.astype(BF16)
    ra = lax.broadcasted_iota(jnp.int32, (128, 256), 0)
    rb = lax.broadcasted_iota(jnp.int32, (128, 256), 1)
    before = ((ra < rb) | (rb >= 128)).astype(BF16)
    counts = jnp.dot(
        jnp.concatenate([member16[:, 128 * i : 128 * i + 128] for i in range(count // 128)], axis=0),
        before,
        preferred_element_type=F32,
    )
    base = jnp.zeros((nk, 128), F32)
    ranks = []
    for i in range(count // 128):
        here = counts[nk * i : nk * i + nk]
        ranks.append(
            jnp.sum(member[:, 128 * i : 128 * i + 128] * (base + here[:, 0:128]), axis=0, keepdims=True)
        )
        base = base + here[:, 128:256]
    rank = jnp.concatenate(ranks, axis=1).astype(jnp.int32)
    placed = (lax.broadcasted_iota(jnp.int32, (128, count), 0) == rank).astype(F32)
    d1, d2, d3 = split3(density)
    compact = jnp.zeros((nk, 128), F32)
    for d in (d1, d2, d3):
        compact += lax.dot_general(member16, (placed * d).astype(BF16), NT, preferred_element_type=F32)
    lane = lax.broadcasted_iota(jnp.int32, (nk, 128), 1)
    compact = jnp.where(lane == 32, jnp.sum(density), compact)
    compact = jnp.where(lane == 33, live[0].astype(F32), compact)
    both = jnp.transpose(jnp.concatenate([stacked(inv_sum), stacked(ca_sum)], axis=0))
    sums_out[:, 0, :] = both[0:64]
    sums_out[:, 1, :] = both[64:128]
    dens = stacked(jnp.broadcast_to(density, (8, count)))
    turned = jnp.transpose(jnp.concatenate([dens, stacked(w)], axis=0))
    sums_out[:, 2, :] = jnp.concatenate([turned[0:64, 0:64], turned[64:128, 0:64]], axis=1)
    sums_out[:, 3, :] = compact
    own[...] = jnp.concatenate([turned[0:64, 64:128], turned[64:128, 64:128]], axis=1)
    mine = (placed * (shard_of == shard).astype(F32)).astype(BF16)
    x1, x2, x3 = split3(jnp.concatenate([w, jnp.broadcast_to((slot_of + 1).astype(F32), (8, count))], axis=0))
    rows = jnp.zeros((16, 128), F32)
    for x in (x1, x2, x3):
        rows += lax.dot_general(x.astype(BF16), mine, NT, preferred_element_type=F32)
    rows_out[0:16, :] = rows
    rows_out[16:24, :] = jnp.broadcast_to(own[pl.ds(shard, 1), :], (8, 128))


def results_kernel(got, rows, norm, results_out, merge_out):
    block = lax.axis_index(WALK)
    total = jnp.sum(got[...], axis=0)
    live_total = total[3:4, 33:34]
    norm_value = norm[0]
    coords = rows[16:17, :]
    lane = lax.broadcasted_iota(jnp.int32, (1, 128), 1)
    first = lane < 64
    inv_sum = jnp.where(first, total[0:1], pltpu.roll(total[1:2], 64, 1))
    ca_sum = jnp.where(first, pltpu.roll(total[0:1], 64, 1), total[1:2])
    both = jnp.concatenate([total[2:3], total[3:4]], axis=0) / live_total
    ratio = both / norm_value + EPSILON
    bias = PREFACTOR * jnp.log(ratio)
    weight = jnp.exp(bias[1:2])
    grad = (-coords * inv_sum + ca_sum) / live_total
    force = -PREFACTOR * grad / (norm_value * ratio[0:1])
    out = jnp.concatenate([force, bias[0:1]], axis=0)
    results_out[...] = jnp.broadcast_to(out[None], results_out.shape)
    shift = 32 * (block % 4)
    weight = jnp.where(lane < 32, weight, 0.0)
    share = jnp.where(lane == 32, both[1:2], 0.0)
    tail = jnp.concatenate(
        [rows[8:9, :], weight, jnp.broadcast_to(jnp.sum(share, axis=1, keepdims=True), (1, 128)),
         jnp.zeros((5, 128), F32)], axis=0)
    packed = jnp.concatenate([rows[0:8, :], tail], axis=0)
    packed = pltpu.roll(packed, shift, 1)
    merge_out[...] = packed


def merge_kernel(walker_count, got, centers, sigmas, heights, sigma_new, norm,
                 heights_out, centers_out, sigmas_out, norm_out):
    kernels = centers.shape[1]
    first = got[0] + got[1] + got[2] + got[3]
    second = got[4] + got[5] + got[6] + got[7]
    cand = jnp.concatenate([first, second], axis=1)
    x = cand[0:8]
    slot = cand[8:9].astype(jnp.int32) - 1
    weight = cand[9:10]
    density_sum = first[10:11, 0:1] + second[10:11, 0:1]
    placing = (lax.broadcasted_iota(jnp.int32, (kernels, 256), 0) == slot).astype(BF16)
    c = centers[...]
    at = jnp.zeros((8, 256), F32)
    for part in split3(c):
        at += jnp.dot(part.astype(BF16), placing, preferred_element_type=F32)
    offset = x - at
    sub = lax.broadcasted_iota(jnp.int32, (8, 1), 0)
    sn = jnp.zeros((8, 1), F32)
    for d in range(8):
        sn = jnp.where(sub == d, sigma_new[d], sn)
    feat = jnp.concatenate(
        [jnp.broadcast_to(weight, (8, 256)), weight * offset, weight * (offset * offset + sn * sn)], axis=0
    )
    sums = jnp.zeros((24, kernels), F32)
    for part in split3(feat):
        sums += lax.dot_general(part.astype(BF16), placing, NT, preferred_element_type=F32)
    h = as_row(heights[...])
    new_h = h + sums[0:1]
    delta = sums[8:16] / new_h
    s = sigmas[...]
    centers_out[...] = c + delta
    sigmas_out[...] = jnp.sqrt((h * s * s + sums[16:24]) / new_h - delta * delta)
    heights_out[...] = jnp.concatenate([new_h[:, 128 * r : 128 * r + 128] for r in range(kernels // 128)], axis=0)
    norm_out[...] = jnp.log((1.0 - RATE) * norm[0] + RATE * density_sum / walker_count)


def spread_kernel(got, bias_out, force_out):
    for row, out in ((0, force_out), (1, None)):
        v = got[:, row, :]
        v = jnp.concatenate([v[:, 0:64], v[:, 64:128]], axis=0)
        v = jnp.concatenate([v, jnp.zeros((128, 64), F32)], axis=1)
        v = jnp.transpose(v)
        for g in range(8):
            if row == 0:
                out[:, 128 * g : 128 * g + 128] = v[8 * g : 8 * g + 8]
            else:
                bias_out[g : g + 1, :] = v[8 * g : 8 * g + 1]


def call(kernel, outs, specs, scratch=(), cost=None, limit=16 * 2**20):
    many = isinstance(outs, (list, tuple))
    return pl.pallas_call(
        kernel,
        out_shape=outs,
        in_specs=specs,
        out_specs=[VMEM] * len(outs) if many else VMEM,
        scratch_shapes=list(scratch),
        cost_estimate=cost,
        compiler_params=pltpu.CompilerParams(vmem_limit_bytes=limit),
    )


def shape(*dims):
    return jax.ShapeDtypeStruct(dims, F32)


def per_device(walkers, centers, sigmas, heights, kernel_live, merge_target, new_sigma, norm_old):
    nk = lax.axis_size("kern")
    nw = lax.axis_size(WALK)
    kernels = centers.shape[1]
    count = walkers.shape[1]
    heights2 = heights.reshape(-1, 128)
    sums, rows = call(
        functools.partial(moments_kernel, BW, BK, nk),
        [shape(nk, 4, 128), shape(24, 128)],
        [HBM, HBM, HBM, HBM, SMEM, HBM],
        [
            pltpu.VMEM((count, 128), BF16),
            pltpu.VMEM((128, kernels), BF16),
            pltpu.VMEM((48, kernels), BF16),
            pltpu.VMEM((nk, 128), F32),
            pltpu.VMEM(walkers.shape, F32),
            pltpu.VMEM(centers.shape, F32),
            pltpu.VMEM(centers.shape, F32),
            pltpu.VMEM(heights2.shape, F32),
            pltpu.VMEM((count // 128, 128), jnp.int32),
            pltpu.SemaphoreType.DMA((5,)),
        ],
        limit=56 * 2**20,
    )(walkers, centers, sigmas, heights2, kernel_live, merge_target.reshape(-1, 128))
    sums = lax.all_to_all(sums, "kern", 0, 0, tiled=True)
    results, packed = call(
        results_kernel,
        [shape(nk, 2, 128), shape(16, 128)],
        [VMEM, VMEM, SMEM],
    )(sums, rows, norm_old)
    results = lax.all_to_all(results, "kern", 0, 0, tiled=True)
    packed = lax.all_gather(lax.all_gather(packed, "wc"), "wx").reshape(nw, 16, 128)
    new_heights, new_centers, new_sigmas, log_norm = call(
        functools.partial(merge_kernel, count * nw),
        [shape(*heights2.shape), shape(*centers.shape), shape(*centers.shape), shape(1, 1)],
        [VMEM, VMEM, VMEM, VMEM, SMEM, SMEM],
        cost=pl.CostEstimate(flops=10**9, bytes_accessed=10**6, transcendentals=0),
    )(packed, centers, sigmas, heights2, new_sigma, norm_old)
    bias, force = call(spread_kernel, [shape(count // 128, 128), shape(8, count)], [VMEM])(results)
    return (
        bias.reshape(-1), force, new_heights.reshape(-1), new_centers, new_sigmas, log_norm.reshape(-1)
    )


BW = 256
BK = 256


def solution(mesh):
    mesh = Mesh(mesh.devices.reshape(mesh.shape["kern"], -1, 2), ("kern", *WALK))
    in_specs = (
        P(None, WALK),
        P(None, "kern"),
        P(None, "kern"),
        P("kern"),
        P("kern"),
        P(WALK),
        P(),
        P(),
    )
    out_specs = (P(WALK), P(None, WALK), P("kern"), P(None, "kern"), P(None, "kern"), P())
    return jax.shard_map(
        per_device, mesh=mesh, in_specs=in_specs, out_specs=out_specs, check_vma=False
    )
```

```python
import functools
import jax
import jax.numpy as jnp
from jax import lax
from jax.experimental import pallas as pl
from jax.experimental.pallas import tpu as pltpu
from jax.sharding import Mesh
from jax.sharding import PartitionSpec as P

WALK = ("wx", "wc")
OWNERS = ("wc", "kern")
PREFACTOR = 0.9
EPSILON = 0.01
RATE = 0.25
LOG2E = 1.4426950408889634
F32 = jnp.float32
BF16 = jnp.bfloat16
NT = (((1,), (1,)), ((), ()))
VMEM = pl.BlockSpec(memory_space=pltpu.VMEM)
HBM = pl.BlockSpec(memory_space=pltpu.HBM)
SMEM = pl.BlockSpec(memory_space=pltpu.SMEM)
BW = 256
BK = 256


def iota(dims, axis):
    return lax.broadcasted_iota(jnp.int32, dims, axis)


def split3(x):
    hi = x.astype(BF16).astype(F32)
    rest = x - hi
    mid = rest.astype(BF16).astype(F32)
    return (hi, mid, rest - mid)


def as_row(x):
    return jnp.concatenate([x[r : r + 1, :] for r in range(x.shape[0])], axis=1)


def blocks(x):
    return [x[:, 128 * g : 128 * g + 128] for g in range(x.shape[1] // 128)]


def moments_kernel(
    nk, walkers_in, centers_in, sigmas_in, heights_in, live, target_in, sums_out, rows_out,
    kt, mom, walkers, centers, sigmas, heights, target, sems,
):
    copies = [
        pltpu.make_async_copy(src, dst, sems.at[n])
        for n, (src, dst) in enumerate((
            (sigmas_in, sigmas), (centers_in, centers), (heights_in, heights), (walkers_in, walkers),
            (target_in, target),
        ))
    ]
    for copy in copies:
        copy.start()
    for copy in copies:
        copy.wait()
    kernels = centers.shape[1]
    count = walkers.shape[1]
    shard = lax.axis_index("kern")
    core = lax.axis_index("wc")
    s = sigmas[...]
    c = centers[...]
    inv = 1.0 / (s * s)
    ca = c * inv
    const = as_row(jnp.log(heights[...])) - 0.5 * jnp.sum(c * ca, axis=0, keepdims=True)
    k1, k2, k3 = split3(jnp.concatenate([(-0.5 * LOG2E) * inv, LOG2E * ca], axis=0))
    c1, c2, c3 = split3(const * LOG2E)
    rows = jnp.concatenate(
        [k1, k2, k3, k1, k2, k1, c1, c2, c3, jnp.zeros((29, kernels), F32)], axis=0
    )
    for n, block in enumerate(blocks(rows)):
        kt[128 * n : 128 * n + 128, :] = jnp.transpose(block).astype(BF16)
    alive = (iota((1, kernels), 1) < live[0]).astype(F32)
    m1, m2, _ = split3(jnp.concatenate([inv, ca], axis=0) * alive)
    mom[...] = jnp.concatenate([m1, m2, alive, jnp.zeros((15, kernels), F32)], axis=0).astype(BF16)
    w = walkers[...]
    w1, w2, w3 = split3(jnp.concatenate([w * w, w], axis=0))
    ones = (iota((32, count), 0) < 3).astype(F32)
    feats = jnp.concatenate([w1, w1, w1, w2, w2, w3, ones], axis=0).astype(BF16)
    parts = []
    for i in range(count // BW):
        right = feats[:, BW * i : BW * i + BW]
        total = jnp.zeros((48, BW), F32)
        for j in range(kernels // BK):
            expo = jnp.dot(kt[BK * j : BK * j + BK], right, preferred_element_type=F32)
            e = jnp.exp2(expo)
            e1 = e.astype(BF16)
            e2 = (e - e1.astype(F32)).astype(BF16)
            m = mom[:, BK * j : BK * j + BK]
            total += jnp.dot(m, e1, preferred_element_type=F32)
            total += jnp.dot(m, e2, preferred_element_type=F32)
        parts.append(total)
    summed = jnp.concatenate(parts, axis=1)
    density = summed[32:33]
    slope = (summed[8:16] + summed[24:32]) - w * (summed[0:8] + summed[16:24])
    t = as_row(target[...])
    shard_of = t // kernels
    slot_of = t - shard_of * kernels
    member = (iota((nk, count), 0) == shard_of).astype(F32)
    member16 = member.astype(BF16)
    ra = iota((128, 256), 0)
    rb = iota((128, 256), 1)
    before = ((ra < rb) | (rb >= 128)).astype(BF16)
    counts = jnp.dot(jnp.concatenate(blocks(member16), axis=0), before, preferred_element_type=F32)
    base = jnp.zeros((nk, 128), F32)
    ranks = []
    for n, block in enumerate(blocks(member)):
        here = counts[nk * n : nk * n + nk]
        ranks.append(jnp.sum(block * (base + here[:, 0:128]), axis=0, keepdims=True))
        base = base + here[:, 128:256]
    rank = jnp.concatenate(ranks, axis=1).astype(jnp.int32)
    lane_of = 8 * (rank % 8) + rank // 8
    placed = (iota((64, count), 0) == lane_of + 1).astype(F32)
    d1, d2, d3 = split3(density)
    terms = jnp.concatenate([placed * d3, placed * d1, placed * d2, jnp.zeros((64, count), F32)], axis=0)
    compact = lax.dot_general(member16, terms.astype(BF16), NT, preferred_element_type=F32)
    near = compact[:, 0:128]
    compact = near + pltpu.roll(near, 64, 1) + pltpu.roll(compact[:, 128:256], 64, 1)
    lane = iota((nk, 128), 1)
    compact = jnp.where(lane < 64, 0.0, compact)
    compact = jnp.where(lane == 69, jnp.sum(density), compact)
    compact = jnp.where(lane == 77, live[0].astype(F32), compact)
    first = (iota((8, 1), 0) == 0).astype(F32)
    turned = jnp.transpose(jnp.concatenate(blocks(slope) + blocks(density * first), axis=0))
    sums_out[...] = turned + jnp.concatenate([compact, compact], axis=0)
    mine = (iota((64, count), 0) == lane_of + 4 * core) & (shard_of == shard)
    mine = jnp.concatenate([mine.astype(F32), jnp.zeros((64, count), F32)], axis=0).astype(BF16)
    x = jnp.concatenate([w, jnp.broadcast_to((slot_of + 1).astype(F32), (8, count))], axis=0)
    picked = lax.dot_general(
        jnp.concatenate(split3(x), axis=0).astype(BF16), mine, NT, preferred_element_type=F32
    )
    rows_out[...] = picked[0:16] + picked[16:32] + picked[32:48]


def results_kernel(got, rows, norm, results_out, merge_out):
    half = got.shape[0] // 2
    total = jnp.concatenate(
        [jnp.sum(got[0:half], axis=0, keepdims=True), jnp.sum(got[half : 2 * half], axis=0, keepdims=True)],
        axis=0,
    )
    live_total = total[0:1, 77:78]
    norm_value = norm[0]
    lane = iota((2, 128), 1)
    low = lane < 64
    wide = jnp.where((lane % 8 == 0) & (lane >= 64), total, 0.0)
    for step in (1, 2, 4):
        wide = wide + pltpu.roll(wide, step, 1)
    density = jnp.where(low, pltpu.roll(wide, 64, 1), total) / live_total
    ratio = density / norm_value + EPSILON
    bias = PREFACTOR * jnp.log(ratio)
    weight = jnp.exp(bias)
    force = -PREFACTOR * (total / live_total) / (norm_value * ratio)
    out = jnp.where(low, force, bias)
    for n in range(2):
        results_out[half * n : half * n + half, :] = jnp.broadcast_to(out[n : n + 1], (half, 128))
    place = lane % 8
    weight = jnp.where((lane >= 64) & (place >= 1) & (place <= 4), weight, 0.0)
    weight = pltpu.roll(weight[0:1], 63, 1) + pltpu.roll(weight[1:2], 67, 1)
    share = jnp.sum(jnp.where(lane == 69, density, 0.0))
    share = jnp.where(lane[0:1] == 0, share, 0.0)
    known = rows[0] + rows[1]
    packed = jnp.concatenate([known[0:9], weight, share, jnp.zeros((5, 128), F32)], axis=0)
    merge_out[...] = pltpu.roll(packed, 64 * (lax.axis_index("wx") % 2), 1)


def merge_kernel(walker_count, got, centers, sigmas, heights, sigma_new, norm,
                 heights_out, centers_out, sigmas_out, norm_out):
    kernels = centers.shape[1]
    cand = jnp.concatenate([got[0] + got[1], got[2] + got[3]], axis=1)
    x = cand[0:8]
    slot = cand[8:9].astype(jnp.int32) - 1
    weight = cand[9:10]
    density_sum = jnp.sum(cand[10:11], axis=1, keepdims=True)
    placing = (iota((kernels, cand.shape[1]), 0) == slot).astype(BF16)
    c = centers[...]
    at = jnp.dot(jnp.concatenate(split3(c), axis=0).astype(BF16), placing, preferred_element_type=F32)
    offset = x - (at[0:8] + at[8:16] + at[16:24])
    sub = iota((8, 1), 0)
    sn = jnp.zeros((8, 1), F32)
    for d in range(8):
        sn = jnp.where(sub == d, sigma_new[d], sn)
    feat = jnp.concatenate(
        [jnp.broadcast_to(weight, x.shape), weight * offset, weight * (offset * offset + sn * sn)], axis=0
    )
    sums = lax.dot_general(
        jnp.concatenate(split3(feat), axis=0).astype(BF16), placing, NT, preferred_element_type=F32
    )
    sums = sums[0:24] + sums[24:48] + sums[48:72]
    h = as_row(heights[...])
    new_h = h + sums[0:1]
    delta = sums[8:16] / new_h
    s = sigmas[...]
    centers_out[...] = c + delta
    sigmas_out[...] = jnp.sqrt((h * s * s + sums[16:24]) / new_h - delta * delta)
    heights_out[...] = jnp.concatenate(blocks(new_h), axis=0)
    norm_out[...] = jnp.log((1.0 - RATE) * norm[0] + RATE * density_sum / walker_count)


def spread_kernel(got, bias_out, force_out):
    turned = jnp.transpose(got[...])
    for g in range(8):
        force_out[:, 128 * g : 128 * g + 128] = turned[8 * g : 8 * g + 8]
        bias_out[g : g + 1, :] = turned[64 + 8 * g : 65 + 8 * g]


def call(kernel, outs, specs, scratch=(), limit=16 * 2**20):
    return pl.pallas_call(
        kernel,
        out_shape=outs,
        in_specs=specs,
        out_specs=[VMEM] * len(outs),
        scratch_shapes=list(scratch),
        compiler_params=pltpu.CompilerParams(vmem_limit_bytes=limit),
    )


def shape(*dims):
    return jax.ShapeDtypeStruct(dims, F32)


def per_device(walkers, centers, sigmas, heights, kernel_live, merge_target, new_sigma, norm_old):
    nk = lax.axis_size("kern")
    nw = lax.axis_size(WALK)
    kernels = centers.shape[1]
    count = walkers.shape[1]
    heights2 = heights.reshape(-1, 128)
    sums, rows = call(
        functools.partial(moments_kernel, nk),
        [shape(2 * nk, 128), shape(16, 128)],
        [HBM, HBM, HBM, HBM, SMEM, HBM],
        [
            pltpu.VMEM((kernels, 128), BF16),
            pltpu.VMEM((48, kernels), BF16),
            pltpu.VMEM(walkers.shape, F32),
            pltpu.VMEM(centers.shape, F32),
            pltpu.VMEM(centers.shape, F32),
            pltpu.VMEM(heights2.shape, F32),
            pltpu.VMEM((count // 128, 128), jnp.int32),
            pltpu.SemaphoreType.DMA((5,)),
        ],
        limit=56 * 2**20,
    )(walkers, centers, sigmas, heights2, kernel_live, merge_target.reshape(-1, 128))
    sums = lax.all_to_all(sums, OWNERS, 0, 0, tiled=True)
    rows = lax.all_gather(rows, "wc")
    results, packed = call(
        results_kernel,
        [shape(2 * nk, 128), shape(16, 128)],
        [VMEM, VMEM, SMEM],
    )(sums, rows, norm_old)
    results = lax.all_to_all(results, OWNERS, 0, 0, tiled=True)
    packed = lax.all_gather(packed, "wx")
    new_heights, new_centers, new_sigmas, log_norm = call(
        functools.partial(merge_kernel, count * nw),
        [shape(*heights2.shape), shape(*centers.shape), shape(*centers.shape), shape(1, 1)],
        [VMEM, VMEM, VMEM, VMEM, SMEM, SMEM],
    )(packed, centers, sigmas, heights2, new_sigma, norm_old)
    bias, force = call(spread_kernel, [shape(count // 128, 128), shape(8, count)], [VMEM])(results)
    return (
        bias.reshape(-1), force, new_heights.reshape(-1), new_centers, new_sigmas, log_norm.reshape(-1)
    )


def solution(mesh):
    mesh = Mesh(mesh.devices.reshape(mesh.shape["kern"], -1, 2), ("kern", *WALK))
    in_specs = (
        P(None, WALK),
        P(None, "kern"),
        P(None, "kern"),
        P("kern"),
        P("kern"),
        P(WALK),
        P(),
        P(),
    )
    out_specs = (P(WALK), P(None, WALK), P("kern"), P(None, "kern"), P(None, "kern"), P())
    return jax.shard_map(
        per_device, mesh=mesh, in_specs=in_specs, out_specs=out_specs, check_vma=False
    )
```

```python
import functools
import jax
import jax.numpy as jnp
from jax import lax
from jax.experimental import pallas as pl
from jax.experimental.pallas import tpu as pltpu
from jax.sharding import Mesh
from jax.sharding import PartitionSpec as P

WALK = ("wx", "wc")
OWNERS = ("wc", "kern")
PREFACTOR = 0.9
EPSILON = 0.01
RATE = 0.25
LOG2E = 1.4426950408889634
F32 = jnp.float32
BF16 = jnp.bfloat16
NT = (((1,), (1,)), ((), ()))
VMEM = pl.BlockSpec(memory_space=pltpu.VMEM)
SMEM = pl.BlockSpec(memory_space=pltpu.SMEM)
HBM = pl.BlockSpec(memory_space=pltpu.HBM)
BW = 256
BK = 256


def iota(dims, axis):
    return lax.broadcasted_iota(jnp.int32, dims, axis)


def split3(x):
    hi = x.astype(BF16).astype(F32)
    rest = x - hi
    mid = rest.astype(BF16).astype(F32)
    return (hi, mid, rest - mid)


def as_row(x):
    return jnp.concatenate([x[r : r + 1, :] for r in range(x.shape[0])], axis=1)


def blocks(x):
    return [x[:, 128 * g : 128 * g + 128] for g in range(x.shape[1] // 128)]


def moments_kernel(
    nk, walkers_in, centers_in, sigmas_in, heights_in, live_in, target_in, new_in,
    sums_out, rows_out, consts_out,
    kt, mom, walkers, centers, sigmas, heights, target, live, new, sems,
):
    copies = [
        pltpu.make_async_copy(src, dst, sems.at[n])
        for n, (src, dst) in enumerate((
            (sigmas_in, sigmas), (centers_in, centers), (heights_in, heights), (walkers_in, walkers),
            (target_in, target), (live_in, live), (new_in, new),
        ))
    ]
    for copy in copies:
        copy.start()
    for copy in copies:
        copy.wait()
    kernels = centers.shape[1]
    count = walkers.shape[1]
    shard = lax.axis_index("kern")
    core = lax.axis_index("wc")
    s = sigmas[...]
    c = centers[...]
    inv = 1.0 / (s * s)
    ca = c * inv
    const = as_row(jnp.log(heights[...])) - 0.5 * jnp.sum(c * ca, axis=0, keepdims=True)
    k1, k2, k3 = split3(jnp.concatenate([(-0.5 * LOG2E) * inv, LOG2E * ca], axis=0))
    c1, c2, c3 = split3(const * LOG2E)
    rows = jnp.concatenate(
        [k1, k2, k3, k1, k2, k1, c1, c2, c3, jnp.zeros((29, kernels), F32)], axis=0
    )
    for n, block in enumerate(blocks(rows)):
        kt[128 * n : 128 * n + 128, :] = jnp.transpose(block).astype(BF16)
    alive = (iota((1, kernels), 1) < live[0]).astype(F32)
    m1, m2, _ = split3(jnp.concatenate([inv, ca], axis=0) * alive)
    mom[...] = jnp.concatenate([m1, m2, alive, jnp.zeros((15, kernels), F32)], axis=0).astype(BF16)
    w = walkers[...]
    w1, w2, w3 = split3(jnp.concatenate([w * w, w], axis=0))
    ones = (iota((32, count), 0) < 3).astype(F32)
    feats = jnp.concatenate([w1, w1, w1, w2, w2, w3, ones], axis=0).astype(BF16)
    parts = []
    for i in range(count // BW):
        right = feats[:, BW * i : BW * i + BW]
        total = jnp.zeros((48, BW), F32)
        for j in range(kernels // BK):
            expo = jnp.dot(kt[BK * j : BK * j + BK], right, preferred_element_type=F32)
            e = jnp.exp2(expo)
            e1 = e.astype(BF16)
            e2 = (e - e1.astype(F32)).astype(BF16)
            m = mom[:, BK * j : BK * j + BK]
            total += jnp.dot(m, e1, preferred_element_type=F32)
            total += jnp.dot(m, e2, preferred_element_type=F32)
        parts.append(total)
    summed = jnp.concatenate(parts, axis=1)
    density = summed[32:33]
    slope = (summed[8:16] + summed[24:32]) - w * (summed[0:8] + summed[16:24])
    t = as_row(target[...])
    shard_of = t // kernels
    slot_of = t - shard_of * kernels
    member = (iota((nk, count), 0) == shard_of).astype(F32)
    member16 = member.astype(BF16)
    ra = iota((128, 256), 0)
    rb = iota((128, 256), 1)
    before = ((ra < rb) | (rb >= 128)).astype(BF16)
    counts = jnp.dot(jnp.concatenate(blocks(member16), axis=0), before, preferred_element_type=F32)
    base = jnp.zeros((nk, 128), F32)
    ranks = []
    for n, block in enumerate(blocks(member)):
        here = counts[nk * n : nk * n + nk]
        ranks.append(jnp.sum(block * (base + here[:, 0:128]), axis=0, keepdims=True))
        base = base + here[:, 128:256]
    rank = jnp.concatenate(ranks, axis=1).astype(jnp.int32)
    lane_of = 8 * (rank % 8) + rank // 8
    placed = (iota((64, count), 0) == lane_of + 1).astype(F32)
    d1, d2, d3 = split3(density)
    terms = jnp.concatenate([placed * d3, placed * d1, placed * d2, jnp.zeros((64, count), F32)], axis=0)
    compact = lax.dot_general(member16, terms.astype(BF16), NT, preferred_element_type=F32)
    near = compact[:, 0:128]
    compact = near + pltpu.roll(near, 64, 1) + pltpu.roll(compact[:, 128:256], 64, 1)
    lane = iota((nk, 128), 1)
    compact = jnp.where(lane < 64, 0.0, compact)
    compact = jnp.where(lane == 69, jnp.sum(density), compact)
    compact = jnp.where(lane == 77, live[0].astype(F32), compact)
    first = (iota((8, 1), 0) == 0).astype(F32)
    turned = jnp.transpose(jnp.concatenate(blocks(slope) + blocks(density * first), axis=0))
    sums_out[...] = turned + jnp.concatenate([compact, compact], axis=0)
    mine = (iota((64, count), 0) == lane_of + 4 * core) & (shard_of == shard)
    mine = jnp.concatenate([mine.astype(F32), jnp.zeros((64, count), F32)], axis=0).astype(BF16)
    x = jnp.concatenate([w, jnp.broadcast_to((slot_of + 1).astype(F32), (8, count))], axis=0)
    picked = lax.dot_general(
        jnp.concatenate(split3(x), axis=0).astype(BF16), mine, NT, preferred_element_type=F32
    )
    rows_out[...] = picked[0:16] + picked[16:32] + picked[32:48]
    sub = iota((8, 128), 0)
    widths = jnp.zeros((8, 128), F32)
    for d in range(8):
        widths = jnp.where(sub == d, new[d], widths)
    consts_out[...] = widths


def results_kernel(got, rows, norm, results_out, merge_out):
    half = got.shape[0] // 2
    total = jnp.concatenate(
        [jnp.sum(got[0:half], axis=0, keepdims=True), jnp.sum(got[half : 2 * half], axis=0, keepdims=True)],
        axis=0,
    )
    live_total = total[0:1, 77:78]
    norm_value = norm[0]
    lane = iota((2, 128), 1)
    low = lane < 64
    wide = jnp.where((lane % 8 == 0) & (lane >= 64), total, 0.0)
    for step in (1, 2, 4):
        wide = wide + pltpu.roll(wide, step, 1)
    density = jnp.where(low, pltpu.roll(wide, 64, 1), total) / live_total
    ratio = density / norm_value + EPSILON
    bias = PREFACTOR * jnp.log(ratio)
    weight = jnp.exp(bias)
    force = -PREFACTOR * (total / live_total) / (norm_value * ratio)
    out = jnp.where(low, force, bias)
    for n in range(2):
        results_out[half * n : half * n + half, :] = jnp.broadcast_to(out[n : n + 1], (half, 128))
    place = lane % 8
    weight = jnp.where((lane >= 64) & (place >= 1) & (place <= 4), weight, 0.0)
    weight = pltpu.roll(weight[0:1], 63, 1) + pltpu.roll(weight[1:2], 67, 1)
    share = jnp.sum(jnp.where(lane == 69, density, 0.0))
    share = jnp.where(lane[0:1] == 0, share, 0.0)
    known = rows[0] + rows[1]
    packed = jnp.concatenate([known[0:9], weight, share, jnp.zeros((5, 128), F32)], axis=0)
    merge_out[...] = pltpu.roll(packed, 64 * (lax.axis_index("wx") % 2), 1)


def merge_kernel(walker_count, got, centers, sigmas, heights, consts, norm,
                 heights_out, centers_out, sigmas_out, norm_out):
    kernels = centers.shape[1]
    cand = jnp.concatenate([got[0] + got[1], got[2] + got[3]], axis=1)
    x = cand[0:8]
    slot = cand[8:9].astype(jnp.int32) - 1
    weight = cand[9:10]
    density_sum = jnp.sum(cand[10:11], axis=1, keepdims=True)
    placing = (iota((kernels, cand.shape[1]), 0) == slot).astype(BF16)
    c = centers[...]
    at = jnp.dot(jnp.concatenate(split3(c), axis=0).astype(BF16), placing, preferred_element_type=F32)
    offset = x - (at[0:8] + at[8:16] + at[16:24])
    sn = consts[0:8, 0:1]
    feat = jnp.concatenate(
        [jnp.broadcast_to(weight, x.shape), weight * offset, weight * (offset * offset + sn * sn)], axis=0
    )
    sums = lax.dot_general(
        jnp.concatenate(split3(feat), axis=0).astype(BF16), placing, NT, preferred_element_type=F32
    )
    sums = sums[0:24] + sums[24:48] + sums[48:72]
    h = as_row(heights[...])
    new_h = h + sums[0:1]
    delta = sums[8:16] / new_h
    s = sigmas[...]
    centers_out[...] = c + delta
    sigmas_out[...] = jnp.sqrt((h * s * s + sums[16:24]) / new_h - delta * delta)
    heights_out[...] = jnp.concatenate(blocks(new_h), axis=0)
    norm_out[...] = jnp.log((1.0 - RATE) * norm[0] + RATE * density_sum / walker_count)


def spread_kernel(got, bias_out, force_out):
    turned = jnp.transpose(got[...])
    for g in range(8):
        force_out[:, 128 * g : 128 * g + 128] = turned[8 * g : 8 * g + 8]
        bias_out[g : g + 1, :] = turned[64 + 8 * g : 65 + 8 * g]


def call(kernel, outs, specs, scratch=(), limit=16 * 2**20):
    return pl.pallas_call(
        kernel,
        out_shape=outs,
        in_specs=specs,
        out_specs=[VMEM] * len(outs),
        scratch_shapes=list(scratch),
        compiler_params=pltpu.CompilerParams(vmem_limit_bytes=limit),
    )


def shape(*dims):
    return jax.ShapeDtypeStruct(dims, F32)


def per_device(walkers, centers, sigmas, heights, kernel_live, merge_target, new_sigma, norm_old):
    nk = lax.axis_size("kern")
    nw = lax.axis_size(WALK)
    kernels = centers.shape[1]
    count = walkers.shape[1]
    heights2 = heights.reshape(-1, 128)
    sums, rows, consts = call(
        functools.partial(moments_kernel, nk),
        [shape(2 * nk, 128), shape(16, 128), shape(8, 128)],
        [HBM] * 7,
        [
            pltpu.VMEM((kernels, 128), BF16),
            pltpu.VMEM((48, kernels), BF16),
            pltpu.VMEM(walkers.shape, F32),
            pltpu.VMEM(centers.shape, F32),
            pltpu.VMEM(centers.shape, F32),
            pltpu.VMEM(heights2.shape, F32),
            pltpu.VMEM((count // 128, 128), jnp.int32),
            pltpu.SMEM(kernel_live.shape, jnp.int32),
            pltpu.SMEM(new_sigma.shape, F32),
            pltpu.SemaphoreType.DMA((7,)),
        ],
        limit=56 * 2**20,
    )(walkers, centers, sigmas, heights2, kernel_live, merge_target.reshape(-1, 128), new_sigma)
    sums = lax.all_to_all(sums, OWNERS, 0, 0, tiled=True)
    rows = lax.all_gather(rows, "wc")
    results, packed = call(
        results_kernel,
        [shape(2 * nk, 128), shape(16, 128)],
        [VMEM, VMEM, SMEM],
    )(sums, rows, norm_old)
    results = lax.all_to_all(results, OWNERS, 0, 0, tiled=True)
    packed = lax.all_gather(packed, "wx")
    new_heights, new_centers, new_sigmas, log_norm = call(
        functools.partial(merge_kernel, count * nw),
        [shape(*heights2.shape), shape(*centers.shape), shape(*centers.shape), shape(1, 1)],
        [VMEM, VMEM, VMEM, VMEM, VMEM, SMEM],
    )(packed, centers, sigmas, heights2, consts, norm_old)
    bias, force = call(spread_kernel, [shape(count // 128, 128), shape(8, count)], [VMEM])(results)
    return (
        bias.reshape(-1), force, new_heights.reshape(-1), new_centers, new_sigmas, log_norm.reshape(-1)
    )


def solution(mesh):
    mesh = Mesh(mesh.devices.reshape(mesh.shape["kern"], -1, 2), ("kern", *WALK))
    in_specs = (
        P(None, WALK),
        P(None, "kern"),
        P(None, "kern"),
        P("kern"),
        P("kern"),
        P(WALK),
        P(),
        P(),
    )
    out_specs = (P(WALK), P(None, WALK), P("kern"), P(None, "kern"), P(None, "kern"), P())
    return jax.shard_map(
        per_device, mesh=mesh, in_specs=in_specs, out_specs=out_specs, check_vma=False
    )
```

```python
import functools
import jax
import jax.numpy as jnp
from jax import lax
from jax.experimental import pallas as pl
from jax.experimental.pallas import tpu as pltpu
from jax.sharding import Mesh
from jax.sharding import PartitionSpec as P

WALK = ("wx", "wc")
PREFACTOR = 0.9
EPSILON = 0.01
RATE = 0.25
LOG2E = 1.4426950408889634
F32 = jnp.float32
BF16 = jnp.bfloat16
NT = (((1,), (1,)), ((), ()))
VMEM = pl.BlockSpec(memory_space=pltpu.VMEM)
SMEM = pl.BlockSpec(memory_space=pltpu.SMEM)
HBM = pl.BlockSpec(memory_space=pltpu.HBM)
BW = 256
BK = 256


def iota(dims, axis):
    return lax.broadcasted_iota(jnp.int32, dims, axis)


def split3(x):
    hi = x.astype(BF16).astype(F32)
    rest = x - hi
    mid = rest.astype(BF16).astype(F32)
    return (hi, mid, rest - mid)


def as_row(x):
    return jnp.concatenate([x[r : r + 1, :] for r in range(x.shape[0])], axis=1)


def blocks(x):
    return [x[:, 128 * g : 128 * g + 128] for g in range(x.shape[1] // 128)]


def moments_kernel(
    nk, walkers_in, centers_in, sigmas_in, heights_in, live_in, target_in, new_in,
    sums_out, rows_out, consts_out,
    kt, mom, walkers, centers, sigmas, heights, target, live, new, sems,
):
    copies = [
        pltpu.make_async_copy(src, dst, sems.at[n])
        for n, (src, dst) in enumerate((
            (sigmas_in, sigmas), (centers_in, centers), (heights_in, heights), (walkers_in, walkers),
            (target_in, target), (live_in, live), (new_in, new),
        ))
    ]
    for copy in copies:
        copy.start()
    for copy in copies:
        copy.wait()
    kernels = centers.shape[1]
    count = walkers.shape[1]
    shard = lax.axis_index("kern")
    s = sigmas[...]
    c = centers[...]
    inv = 1.0 / (s * s)
    ca = c * inv
    const = as_row(jnp.log(heights[...])) - 0.5 * jnp.sum(c * ca, axis=0, keepdims=True)
    k1, k2, k3 = split3(jnp.concatenate([(-0.5 * LOG2E) * inv, LOG2E * ca], axis=0))
    c1, c2, c3 = split3(const * LOG2E)
    rows = jnp.concatenate(
        [k1, k2, k3, k1, k2, k1, c1, c2, c3, jnp.zeros((29, kernels), F32)], axis=0
    )
    for n, block in enumerate(blocks(rows)):
        kt[128 * n : 128 * n + 128, :] = jnp.transpose(block).astype(BF16)
    alive = (iota((1, kernels), 1) < live[0]).astype(F32)
    m1, m2, _ = split3(jnp.concatenate([inv, ca], axis=0) * alive)
    mom[...] = jnp.concatenate([m1, m2, alive, jnp.zeros((15, kernels), F32)], axis=0).astype(BF16)
    w = walkers[...]
    w1, w2, w3 = split3(jnp.concatenate([w * w, w], axis=0))
    ones = (iota((32, count), 0) < 3).astype(F32)
    feats = jnp.concatenate([w1, w1, w1, w2, w2, w3, ones], axis=0).astype(BF16)
    parts = []
    for i in range(count // BW):
        right = feats[:, BW * i : BW * i + BW]
        total = jnp.zeros((48, BW), F32)
        for j in range(kernels // BK):
            expo = jnp.dot(kt[BK * j : BK * j + BK], right, preferred_element_type=F32)
            e = jnp.exp2(expo)
            e1 = e.astype(BF16)
            e2 = (e - e1.astype(F32)).astype(BF16)
            m = mom[:, BK * j : BK * j + BK]
            total += jnp.dot(m, e1, preferred_element_type=F32)
            total += jnp.dot(m, e2, preferred_element_type=F32)
        parts.append(total)
    summed = jnp.concatenate(parts, axis=1)
    density = summed[32:33]
    slope = (summed[8:16] + summed[24:32]) - w * (summed[0:8] + summed[16:24])
    t = as_row(target[...])
    shard_of = t // kernels
    slot_of = t - shard_of * kernels
    member = (iota((nk, count), 0) == shard_of).astype(F32)
    member16 = member.astype(BF16)
    ra = iota((128, 256), 0)
    rb = iota((128, 256), 1)
    before = ((ra < rb) | (rb >= 128)).astype(BF16)
    counts = jnp.dot(jnp.concatenate(blocks(member16), axis=0), before, preferred_element_type=F32)
    base = jnp.zeros((nk, 128), F32)
    ranks = []
    for n, block in enumerate(blocks(member)):
        here = counts[nk * n : nk * n + nk]
        ranks.append(jnp.sum(block * (base + here[:, 0:128]), axis=0, keepdims=True))
        base = base + here[:, 128:256]
    rank = jnp.concatenate(ranks, axis=1).astype(jnp.int32)
    lane_of = 8 * (rank % 8) + rank // 8
    placed = (iota((64, count), 0) == lane_of + 1).astype(F32)
    d1, d2, d3 = split3(density)
    terms = jnp.concatenate([placed * d3, placed * d1, placed * d2, jnp.zeros((64, count), F32)], axis=0)
    compact = lax.dot_general(member16, terms.astype(BF16), NT, preferred_element_type=F32)
    near = compact[:, 0:128]
    compact = near + pltpu.roll(near, 64, 1) + pltpu.roll(compact[:, 128:256], 64, 1)
    lane = iota((nk, 128), 1)
    compact = jnp.where(lane < 64, 0.0, compact)
    compact = jnp.where(lane == 69, jnp.sum(density), compact)
    compact = jnp.where(lane == 77, live[0].astype(F32), compact)
    first = (iota((8, 1), 0) == 0).astype(F32)
    turned = jnp.transpose(jnp.concatenate(blocks(slope) + blocks(density * first), axis=0))
    sums_out[pl.ds(0, nk, stride=2), :] = turned[0:nk] + compact
    sums_out[pl.ds(1, nk, stride=2), :] = turned[nk : 2 * nk]
    mine = (iota((64, count), 0) == lane_of) & (shard_of == shard)
    mine = jnp.concatenate([mine.astype(F32), jnp.zeros((64, count), F32)], axis=0).astype(BF16)
    x = jnp.concatenate([w, jnp.broadcast_to((slot_of + 1).astype(F32), (8, count))], axis=0)
    picked = lax.dot_general(
        jnp.concatenate(split3(x), axis=0).astype(BF16), mine, NT, preferred_element_type=F32
    )
    rows_out[...] = picked[0:16] + picked[16:32] + picked[32:48]
    sub = iota((8, 128), 0)
    widths = jnp.zeros((8, 128), F32)
    for d in range(8):
        widths = jnp.where(sub == d, new[d], widths)
    consts_out[...] = widths


def results_kernel(got, rows, norm, results_out, merge_out):
    total = got[0:8, :]
    for n in range(1, got.shape[0] // 8):
        total = total + got[8 * n : 8 * n + 8, :]
    total = total[0:2] + total[2:4] + total[4:6] + total[6:8]
    live_total = total[0:1, 77:78]
    norm_value = norm[0]
    lane = iota((2, 128), 1)
    low = lane < 64
    wide = jnp.where((lane % 8 == 0) & (lane >= 64), total, 0.0)
    for step in (1, 2, 4):
        wide = wide + pltpu.roll(wide, step, 1)
    density = jnp.where(low, pltpu.roll(wide, 64, 1), total) / live_total
    ratio = density / norm_value + EPSILON
    bias = PREFACTOR * jnp.log(ratio)
    weight = jnp.exp(bias)
    force = -PREFACTOR * (total / live_total) / (norm_value * ratio)
    out = jnp.where(low, force, bias)
    results_out[...] = jnp.concatenate([out] * (got.shape[0] // 2), axis=0)
    place = lane % 8
    weight = jnp.where((lane >= 64) & (place >= 1) & (place <= 4), weight, 0.0)
    weight = pltpu.roll(weight[0:1], 63, 1)
    share = jnp.sum(jnp.where(lane == 69, density, 0.0)[0:1])
    share = jnp.where(lane[0:1] == 0, share, 0.0)
    packed = jnp.concatenate([rows[0:9], weight, share, jnp.zeros((5, 128), F32)], axis=0)
    x = lax.axis_index("wx")
    merge_out[...] = pltpu.roll(packed, 64 * (x % 2) + 4 * (x // 2), 1)


def final_kernel(walker_count, got, results, centers, sigmas, heights, consts, norm,
                 bias_out, force_out, heights_out, centers_out, sigmas_out, norm_out):
    half = results.shape[0] // 2
    turned = jnp.transpose(jnp.concatenate(
        [results[pl.ds(0, half, stride=2), :], results[pl.ds(1, half, stride=2), :]], axis=0
    ))
    for g in range(8):
        force_out[:, 128 * g : 128 * g + 128] = turned[8 * g : 8 * g + 8]
        bias_out[g : g + 1, :] = turned[64 + 8 * g : 65 + 8 * g]
    kernels = centers.shape[1]
    cand = jnp.concatenate([got[0], got[1]], axis=1)
    x = cand[0:8]
    slot = cand[8:9].astype(jnp.int32) - 1
    weight = cand[9:10]
    density_sum = jnp.sum(cand[10:11], axis=1, keepdims=True)
    placing = (iota((kernels, cand.shape[1]), 0) == slot).astype(BF16)
    c = centers[...]
    at = jnp.dot(jnp.concatenate(split3(c), axis=0).astype(BF16), placing, preferred_element_type=F32)
    offset = x - (at[0:8] + at[8:16] + at[16:24])
    sn = consts[0:8, 0:1]
    feat = jnp.concatenate(
        [jnp.broadcast_to(weight, x.shape), weight * offset, weight * (offset * offset + sn * sn)], axis=0
    )
    sums = lax.dot_general(
        jnp.concatenate(split3(feat), axis=0).astype(BF16), placing, NT, preferred_element_type=F32
    )
    sums = sums[0:24] + sums[24:48] + sums[48:72]
    h = as_row(heights[...])
    new_h = h + sums[0:1]
    delta = sums[8:16] / new_h
    s = sigmas[...]
    centers_out[...] = c + delta
    sigmas_out[...] = jnp.sqrt((h * s * s + sums[16:24]) / new_h - delta * delta)
    heights_out[...] = jnp.concatenate(blocks(new_h), axis=0)
    norm_out[...] = jnp.log((1.0 - RATE) * norm[0] + RATE * density_sum / walker_count)


def call(kernel, outs, specs, scratch=(), limit=16 * 2**20):
    return pl.pallas_call(
        kernel,
        out_shape=outs,
        in_specs=specs,
        out_specs=[VMEM] * len(outs),
        scratch_shapes=list(scratch),
        compiler_params=pltpu.CompilerParams(vmem_limit_bytes=limit),
    )


def shape(*dims):
    return jax.ShapeDtypeStruct(dims, F32)


def per_device(walkers, centers, sigmas, heights, kernel_live, merge_target, new_sigma, norm_old):
    nk = lax.axis_size("kern")
    nw = lax.axis_size(WALK)
    kernels = centers.shape[1]
    count = walkers.shape[1]
    heights2 = heights.reshape(-1, 128)
    sums, rows, consts = call(
        functools.partial(moments_kernel, nk),
        [shape(2 * nk, 128), shape(16, 128), shape(8, 128)],
        [HBM] * 7,
        [
            pltpu.VMEM((kernels, 128), BF16),
            pltpu.VMEM((48, kernels), BF16),
            pltpu.VMEM(walkers.shape, F32),
            pltpu.VMEM(centers.shape, F32),
            pltpu.VMEM(centers.shape, F32),
            pltpu.VMEM(heights2.shape, F32),
            pltpu.VMEM((count // 128, 128), jnp.int32),
            pltpu.SMEM(kernel_live.shape, jnp.int32),
            pltpu.SMEM(new_sigma.shape, F32),
            pltpu.SemaphoreType.DMA((7,)),
        ],
        limit=56 * 2**20,
    )(walkers, centers, sigmas, heights2, kernel_live, merge_target.reshape(-1, 128), new_sigma)
    sums = lax.all_to_all(sums.reshape(nk, 2, 128), "kern", 0, 0, tiled=True).reshape(2 * nk, 128)
    results, packed = call(
        results_kernel,
        [shape(2 * nk, 128), shape(16, 128)],
        [VMEM, VMEM, SMEM],
    )(sums, rows, norm_old)
    results = lax.all_to_all(results.reshape(nk, 2, 128), "kern", 0, 0, tiled=True).reshape(2 * nk, 128)
    packed = lax.all_gather(lax.psum(packed, "wx"), "wc")
    bias, force, new_heights, new_centers, new_sigmas, log_norm = call(
        functools.partial(final_kernel, count * nw),
        [
            shape(count // 128, 128), shape(8, count), shape(*heights2.shape), shape(*centers.shape),
            shape(*centers.shape), shape(1, 1),
        ],
        [VMEM, VMEM, VMEM, VMEM, VMEM, VMEM, SMEM],
    )(packed, results, centers, sigmas, heights2, consts, norm_old)
    return (
        bias.reshape(-1), force, new_heights.reshape(-1), new_centers, new_sigmas, log_norm.reshape(-1)
    )


def solution(mesh):
    mesh = Mesh(mesh.devices.reshape(mesh.shape["kern"], -1, 2), ("kern", *WALK))
    in_specs = (
        P(None, WALK),
        P(None, "kern"),
        P(None, "kern"),
        P("kern"),
        P("kern"),
        P(WALK),
        P(),
        P(),
    )
    out_specs = (P(WALK), P(None, WALK), P("kern"), P(None, "kern"), P(None, "kern"), P())
    return jax.shard_map(
        per_device, mesh=mesh, in_specs=in_specs, out_specs=out_specs, check_vma=False
    )
```

```python
import functools
import jax
import jax.numpy as jnp
from jax import lax
from jax.experimental import pallas as pl
from jax.experimental.pallas import tpu as pltpu
from jax.sharding import Mesh
from jax.sharding import PartitionSpec as P

WALK = ("xh", "xl", "wc")
PREFACTOR = 0.9
EPSILON = 0.01
RATE = 0.25
LOG2E = 1.4426950408889634
F32 = jnp.float32
BF16 = jnp.bfloat16
NT = (((1,), (1,)), ((), ()))
VMEM = pl.BlockSpec(memory_space=pltpu.VMEM)
SMEM = pl.BlockSpec(memory_space=pltpu.SMEM)
HBM = pl.BlockSpec(memory_space=pltpu.HBM)
BW = 256
BK = 256


def iota(dims, axis):
    return lax.broadcasted_iota(jnp.int32, dims, axis)


def split3(x):
    hi = x.astype(BF16).astype(F32)
    rest = x - hi
    mid = rest.astype(BF16).astype(F32)
    return (hi, mid, rest - mid)


def as_row(x):
    return jnp.concatenate([x[r : r + 1, :] for r in range(x.shape[0])], axis=1)


def blocks(x):
    return [x[:, 128 * g : 128 * g + 128] for g in range(x.shape[1] // 128)]


def moments_kernel(
    nk, walkers_in, centers_in, sigmas_in, heights_in, live_in, target_in, new_in,
    sums_out, rows_out,
    kt, mom, walkers, centers, sigmas, heights, target, live, new, sems,
):
    copies = [
        pltpu.make_async_copy(src, dst, sems.at[n])
        for n, (src, dst) in enumerate((
            (sigmas_in, sigmas), (centers_in, centers), (heights_in, heights), (walkers_in, walkers),
            (target_in, target), (live_in, live), (new_in, new),
        ))
    ]
    for copy in copies:
        copy.start()
    for copy in copies:
        copy.wait()
    kernels = centers.shape[1]
    count = walkers.shape[1]
    shard = lax.axis_index("kern")
    s = sigmas[...]
    c = centers[...]
    inv = 1.0 / (s * s)
    ca = c * inv
    const = as_row(jnp.log(heights[...])) - 0.5 * jnp.sum(c * ca, axis=0, keepdims=True)
    k1, k2, k3 = split3(jnp.concatenate([(-0.5 * LOG2E) * inv, LOG2E * ca], axis=0))
    c1, c2, c3 = split3(const * LOG2E)
    rows = jnp.concatenate(
        [k1, k2, k3, k1, k2, k1, c1, c2, c3, jnp.zeros((29, kernels), F32)], axis=0
    )
    for n, block in enumerate(blocks(rows)):
        kt[128 * n : 128 * n + 128, :] = jnp.transpose(block).astype(BF16)
    alive = (iota((1, kernels), 1) < live[0]).astype(F32)
    m1, m2, _ = split3(jnp.concatenate([inv, ca], axis=0) * alive)
    mom[...] = jnp.concatenate([m1, m2, alive, jnp.zeros((15, kernels), F32)], axis=0).astype(BF16)
    w = walkers[...]
    w1, w2, w3 = split3(jnp.concatenate([w * w, w], axis=0))
    ones = (iota((32, count), 0) < 3).astype(F32)
    feats = jnp.concatenate([w1, w1, w1, w2, w2, w3, ones], axis=0).astype(BF16)
    parts = []
    for i in range(count // BW):
        right = feats[:, BW * i : BW * i + BW]
        total = jnp.zeros((48, BW), F32)
        for j in range(kernels // BK):
            expo = jnp.dot(kt[BK * j : BK * j + BK], right, preferred_element_type=F32)
            e = jnp.exp2(expo)
            e1 = e.astype(BF16)
            e2 = (e - e1.astype(F32)).astype(BF16)
            m = mom[:, BK * j : BK * j + BK]
            total += jnp.dot(m, e1, preferred_element_type=F32)
            total += jnp.dot(m, e2, preferred_element_type=F32)
        parts.append(total)
    summed = jnp.concatenate(parts, axis=1)
    density = summed[32:33]
    slope = (summed[8:16] + summed[24:32]) - w * (summed[0:8] + summed[16:24])
    t = as_row(target[...])
    shard_of = t // kernels
    slot_of = t - shard_of * kernels
    member = (iota((nk, count), 0) == shard_of).astype(F32)
    member16 = member.astype(BF16)
    ra = iota((128, 256), 0)
    rb = iota((128, 256), 1)
    before = ((ra < rb) | (rb >= 128)).astype(BF16)
    counts = jnp.dot(jnp.concatenate(blocks(member16), axis=0), before, preferred_element_type=F32)
    base = jnp.zeros((nk, 128), F32)
    ranks = []
    for n, block in enumerate(blocks(member)):
        here = counts[nk * n : nk * n + nk]
        ranks.append(jnp.sum(block * (base + here[:, 0:128]), axis=0, keepdims=True))
        base = base + here[:, 128:256]
    rank = jnp.concatenate(ranks, axis=1).astype(jnp.int32)
    lane_of = 8 * (rank % 8) + rank // 8
    placed = (iota((64, count), 0) == lane_of + 1).astype(F32)
    d1, d2, d3 = split3(density)
    terms = jnp.concatenate([placed * d3, placed * d1, placed * d2, jnp.zeros((64, count), F32)], axis=0)
    compact = lax.dot_general(member16, terms.astype(BF16), NT, preferred_element_type=F32)
    near = compact[:, 0:128]
    compact = near + pltpu.roll(near, 64, 1) + pltpu.roll(compact[:, 128:256], 64, 1)
    lane = iota((nk, 128), 1)
    compact = jnp.where(lane < 64, 0.0, compact)
    compact = jnp.where(lane == 69, jnp.sum(density), compact)
    compact = jnp.where(lane == 77, live[0].astype(F32), compact)
    first = (iota((8, 1), 0) == 0).astype(F32)
    turned = jnp.transpose(jnp.concatenate(blocks(slope) + blocks(density * first), axis=0))
    sums_out[pl.ds(0, nk, stride=2), :] = turned[0:nk] + compact
    sums_out[pl.ds(1, nk, stride=2), :] = turned[nk : 2 * nk]
    mine = (iota((64, count), 0) == lane_of) & (shard_of == shard)
    mine = jnp.concatenate([mine.astype(F32), jnp.zeros((64, count), F32)], axis=0).astype(BF16)
    x = jnp.concatenate([w, jnp.broadcast_to((slot_of + 1).astype(F32), (8, count))], axis=0)
    picked = lax.dot_general(
        jnp.concatenate(split3(x), axis=0).astype(BF16), mine, NT, preferred_element_type=F32
    )
    lane = iota((1, 128), 1)
    widths = jnp.zeros((1, 128), F32)
    for d in range(8):
        widths = jnp.where(lane == d, new[d], widths)
    picked = picked[0:9] + picked[16:25] + picked[32:41]
    rows_out[...] = jnp.concatenate([picked, widths, jnp.zeros((6, 128), F32)], axis=0)


def results_kernel(got, rows, norm, results_out, merge_out):
    total = got[0:8, :]
    for n in range(1, got.shape[0] // 8):
        total = total + got[8 * n : 8 * n + 8, :]
    total = total[0:2] + total[2:4] + total[4:6] + total[6:8]
    live_total = total[0:1, 77:78]
    norm_value = norm[0]
    lane = iota((2, 128), 1)
    low = lane < 64
    wide = jnp.where((lane % 8 == 0) & (lane >= 64), total, 0.0)
    for step in (1, 2, 4):
        wide = wide + pltpu.roll(wide, step, 1)
    density = jnp.where(low, pltpu.roll(wide, 64, 1), total) / live_total
    ratio = density / norm_value + EPSILON
    bias = PREFACTOR * jnp.log(ratio)
    weight = jnp.exp(bias)
    force = -PREFACTOR * (total / live_total) / (norm_value * ratio)
    out = jnp.where(low, force, bias)
    results_out[...] = jnp.concatenate([out] * (got.shape[0] // 2), axis=0)
    place = lane % 8
    weight = jnp.where((lane >= 64) & (place >= 1) & (place <= 4), weight, 0.0)
    weight = pltpu.roll(weight[0:1], 63, 1)
    share = jnp.sum(jnp.where(lane == 69, density, 0.0)[0:1])
    share = jnp.where(lane[0:1] == 0, share, 0.0)
    packed = jnp.concatenate([rows[0:9], weight, share, rows[9:10], jnp.zeros((4, 128), F32)], axis=0)
    x = 2 * lax.axis_index("xh") + lax.axis_index("xl")
    merge_out[...] = pltpu.roll(packed, 64 * (x % 2) + 4 * (x // 2), 1)


def final_kernel(walker_count, got, results, centers, sigmas, heights, norm,
                 bias_out, force_out, heights_out, centers_out, sigmas_out, norm_out):
    half = results.shape[0] // 2
    turned = jnp.transpose(jnp.concatenate(
        [results[pl.ds(0, half, stride=2), :], results[pl.ds(1, half, stride=2), :]], axis=0
    ))
    for g in range(8):
        force_out[:, 128 * g : 128 * g + 128] = turned[8 * g : 8 * g + 8]
        bias_out[g : g + 1, :] = turned[64 + 8 * g : 65 + 8 * g]
    kernels = centers.shape[1]
    cand = jnp.concatenate([got[0] + got[2] + got[4] + got[6], got[1] + got[3] + got[5] + got[7]], axis=1)
    x = cand[0:8]
    slot = cand[8:9].astype(jnp.int32) - 1
    weight = cand[9:10]
    density_sum = jnp.sum(cand[10:11], axis=1, keepdims=True)
    placing = (iota((kernels, cand.shape[1]), 0) == slot).astype(BF16)
    c = centers[...]
    at = jnp.dot(jnp.concatenate(split3(c), axis=0).astype(BF16), placing, preferred_element_type=F32)
    offset = x - (at[0:8] + at[8:16] + at[16:24])
    sn = jnp.where(iota((8, 128), 0) == iota((8, 128), 1), got[0][11:12], 0.0)
    sn = jnp.sum(sn, axis=1, keepdims=True)
    feat = jnp.concatenate(
        [jnp.broadcast_to(weight, x.shape), weight * offset, weight * (offset * offset + sn * sn)], axis=0
    )
    sums = lax.dot_general(
        jnp.concatenate(split3(feat), axis=0).astype(BF16), placing, NT, preferred_element_type=F32
    )
    sums = sums[0:24] + sums[24:48] + sums[48:72]
    h = as_row(heights[...])
    new_h = h + sums[0:1]
    delta = sums[8:16] / new_h
    s = sigmas[...]
    centers_out[...] = c + delta
    sigmas_out[...] = jnp.sqrt((h * s * s + sums[16:24]) / new_h - delta * delta)
    heights_out[...] = jnp.concatenate(blocks(new_h), axis=0)
    norm_out[...] = jnp.log((1.0 - RATE) * norm[0] + RATE * density_sum / walker_count)


def call(kernel, outs, specs, scratch=(), limit=16 * 2**20):
    return pl.pallas_call(
        kernel,
        out_shape=outs,
        in_specs=specs,
        out_specs=[VMEM] * len(outs),
        scratch_shapes=list(scratch),
        compiler_params=pltpu.CompilerParams(vmem_limit_bytes=limit),
    )


def shape(*dims):
    return jax.ShapeDtypeStruct(dims, F32)


def per_device(walkers, centers, sigmas, heights, kernel_live, merge_target, new_sigma, norm_old):
    nk = lax.axis_size("kern")
    nw = lax.axis_size(WALK)
    kernels = centers.shape[1]
    count = walkers.shape[1]
    heights2 = heights.reshape(-1, 128)
    sums, rows = call(
        functools.partial(moments_kernel, nk),
        [shape(2 * nk, 128), shape(16, 128)],
        [HBM] * 7,
        [
            pltpu.VMEM((kernels, 128), BF16),
            pltpu.VMEM((48, kernels), BF16),
            pltpu.VMEM(walkers.shape, F32),
            pltpu.VMEM(centers.shape, F32),
            pltpu.VMEM(centers.shape, F32),
            pltpu.VMEM(heights2.shape, F32),
            pltpu.VMEM((count // 128, 128), jnp.int32),
            pltpu.SMEM(kernel_live.shape, jnp.int32),
            pltpu.SMEM(new_sigma.shape, F32),
            pltpu.SemaphoreType.DMA((7,)),
        ],
        limit=56 * 2**20,
    )(walkers, centers, sigmas, heights2, kernel_live, merge_target.reshape(-1, 128), new_sigma)
    sums = lax.all_to_all(sums.reshape(nk, 2, 128), "kern", 0, 0, tiled=True).reshape(2 * nk, 128)
    results, packed = call(
        results_kernel,
        [shape(2 * nk, 128), shape(16, 128)],
        [VMEM, VMEM, SMEM],
    )(sums, rows, norm_old)
    results = lax.all_to_all(results.reshape(nk, 2, 128), "kern", 0, 0, tiled=True).reshape(2 * nk, 128)
    packed = lax.all_gather(lax.all_gather(lax.all_gather(packed, "wc"), "xl"), "xh").reshape(8, 16, 128)
    bias, force, new_heights, new_centers, new_sigmas, log_norm = call(
        functools.partial(final_kernel, count * nw),
        [
            shape(count // 128, 128), shape(8, count), shape(*heights2.shape), shape(*centers.shape),
            shape(*centers.shape), shape(1, 1),
        ],
        [VMEM, VMEM, VMEM, VMEM, VMEM, SMEM],
    )(packed, results, centers, sigmas, heights2, norm_old)
    return (
        bias.reshape(-1), force, new_heights.reshape(-1), new_centers, new_sigmas, log_norm.reshape(-1)
    )


def solution(mesh):
    mesh = Mesh(mesh.devices.reshape(mesh.shape["kern"], -1, 2, 2), ("kern", *WALK))
    in_specs = (
        P(None, WALK),
        P(None, "kern"),
        P(None, "kern"),
        P("kern"),
        P("kern"),
        P(WALK),
        P(),
        P(),
    )
    out_specs = (P(WALK), P(None, WALK), P("kern"), P(None, "kern"), P(None, "kern"), P())
    return jax.shard_map(
        per_device, mesh=mesh, in_specs=in_specs, out_specs=out_specs, check_vma=False
    )
```

```python
import functools
import jax
import jax.numpy as jnp
from jax import lax
from jax.experimental import pallas as pl
from jax.experimental.pallas import tpu as pltpu
from jax.sharding import Mesh
from jax.sharding import PartitionSpec as P

WALK = ("wx", "wc")
NEAR = [[0, 1], [2, 3]]
ACROSS = [[0, 3], [1, 2]]
PREFACTOR = 0.9
EPSILON = 0.01
RATE = 0.25
LOG2E = 1.4426950408889634
F32 = jnp.float32
BF16 = jnp.bfloat16
NT = (((1,), (1,)), ((), ()))
VMEM = pl.BlockSpec(memory_space=pltpu.VMEM)
SMEM = pl.BlockSpec(memory_space=pltpu.SMEM)
HBM = pl.BlockSpec(memory_space=pltpu.HBM)
BW = 256
BK = 256


def iota(dims, axis):
    return lax.broadcasted_iota(jnp.int32, dims, axis)


def split3(x):
    hi = x.astype(BF16).astype(F32)
    rest = x - hi
    mid = rest.astype(BF16).astype(F32)
    return (hi, mid, rest - mid)


def as_row(x):
    return jnp.concatenate([x[r : r + 1, :] for r in range(x.shape[0])], axis=1)


def blocks(x):
    return [x[:, 128 * g : 128 * g + 128] for g in range(x.shape[1] // 128)]


def moments_kernel(
    nk, walkers_in, centers_in, sigmas_in, heights_in, live_in, target_in, new_in,
    sums_out, rows_out,
    kt, mom, walkers, centers, sigmas, heights, target, live, new, sems,
):
    copies = [
        pltpu.make_async_copy(src, dst, sems.at[n])
        for n, (src, dst) in enumerate((
            (sigmas_in, sigmas), (centers_in, centers), (heights_in, heights), (walkers_in, walkers),
            (target_in, target), (live_in, live), (new_in, new),
        ))
    ]
    for copy in copies:
        copy.start()
    for copy in copies:
        copy.wait()
    kernels = centers.shape[1]
    count = walkers.shape[1]
    shard = lax.axis_index("kern")
    s = sigmas[...]
    c = centers[...]
    inv = 1.0 / (s * s)
    ca = c * inv
    const = as_row(jnp.log(heights[...])) - 0.5 * jnp.sum(c * ca, axis=0, keepdims=True)
    k1, k2, k3 = split3(jnp.concatenate([(-0.5 * LOG2E) * inv, LOG2E * ca], axis=0))
    c1, c2, c3 = split3(const * LOG2E)
    rows = jnp.concatenate(
        [k1, k2, k3, k1, k2, k1, c1, c2, c3, jnp.zeros((29, kernels), F32)], axis=0
    )
    for n, block in enumerate(blocks(rows)):
        kt[128 * n : 128 * n + 128, :] = jnp.transpose(block).astype(BF16)
    alive = (iota((1, kernels), 1) < live[0]).astype(F32)
    m1, m2, _ = split3(jnp.concatenate([inv, ca], axis=0) * alive)
    mom[...] = jnp.concatenate([m1, m2, alive, jnp.zeros((15, kernels), F32)], axis=0).astype(BF16)
    w = walkers[...]
    w1, w2, w3 = split3(jnp.concatenate([w * w, w], axis=0))
    ones = (iota((32, count), 0) < 3).astype(F32)
    feats = jnp.concatenate([w1, w1, w1, w2, w2, w3, ones], axis=0).astype(BF16)
    parts = []
    for i in range(count // BW):
        right = feats[:, BW * i : BW * i + BW]
        total = jnp.zeros((48, BW), F32)
        for j in range(kernels // BK):
            expo = jnp.dot(kt[BK * j : BK * j + BK], right, preferred_element_type=F32)
            e = jnp.exp2(expo)
            e1 = e.astype(BF16)
            e2 = (e - e1.astype(F32)).astype(BF16)
            m = mom[:, BK * j : BK * j + BK]
            total += jnp.dot(m, e1, preferred_element_type=F32)
            total += jnp.dot(m, e2, preferred_element_type=F32)
        parts.append(total)
    summed = jnp.concatenate(parts, axis=1)
    density = summed[32:33]
    slope = (summed[8:16] + summed[24:32]) - w * (summed[0:8] + summed[16:24])
    t = as_row(target[...])
    shard_of = t // kernels
    slot_of = t - shard_of * kernels
    member = (iota((nk, count), 0) == shard_of).astype(F32)
    member16 = member.astype(BF16)
    ra = iota((128, 256), 0)
    rb = iota((128, 256), 1)
    before = ((ra < rb) | (rb >= 128)).astype(BF16)
    counts = jnp.dot(jnp.concatenate(blocks(member16), axis=0), before, preferred_element_type=F32)
    base = jnp.zeros((nk, 128), F32)
    ranks = []
    for n, block in enumerate(blocks(member)):
        here = counts[nk * n : nk * n + nk]
        ranks.append(jnp.sum(block * (base + here[:, 0:128]), axis=0, keepdims=True))
        base = base + here[:, 128:256]
    rank = jnp.concatenate(ranks, axis=1).astype(jnp.int32)
    lane_of = 8 * (rank % 8) + rank // 8
    placed = (iota((64, count), 0) == lane_of + 1).astype(F32)
    d1, d2, d3 = split3(density)
    terms = jnp.concatenate([placed * d3, placed * d1, placed * d2, jnp.zeros((64, count), F32)], axis=0)
    compact = lax.dot_general(member16, terms.astype(BF16), NT, preferred_element_type=F32)
    near = compact[:, 0:128]
    compact = near + pltpu.roll(near, 64, 1) + pltpu.roll(compact[:, 128:256], 64, 1)
    lane = iota((nk, 128), 1)
    compact = jnp.where(lane < 64, 0.0, compact)
    compact = jnp.where(lane == 69, jnp.sum(density), compact)
    compact = jnp.where(lane == 77, live[0].astype(F32), compact)
    first = (iota((8, 1), 0) == 0).astype(F32)
    turned = jnp.transpose(jnp.concatenate(blocks(slope) + blocks(density * first), axis=0))
    sums_out[pl.ds(0, nk, stride=2), :] = turned[0:nk] + compact
    sums_out[pl.ds(1, nk, stride=2), :] = turned[nk : 2 * nk]
    mine = (iota((64, count), 0) == lane_of) & (shard_of == shard)
    mine = jnp.concatenate([mine.astype(F32), jnp.zeros((64, count), F32)], axis=0).astype(BF16)
    x = jnp.concatenate([w, jnp.broadcast_to((slot_of + 1).astype(F32), (8, count))], axis=0)
    picked = lax.dot_general(
        jnp.concatenate(split3(x), axis=0).astype(BF16), mine, NT, preferred_element_type=F32
    )
    lane = iota((1, 128), 1)
    widths = jnp.zeros((1, 128), F32)
    for d in range(8):
        widths = jnp.where(lane == d, new[d], widths)
    picked = picked[0:9] + picked[16:25] + picked[32:41]
    rows_out[...] = jnp.concatenate([picked, widths, jnp.zeros((6, 128), F32)], axis=0)


def results_kernel(got, rows, norm, results_out, merge_out):
    total = got[0:8, :]
    for n in range(1, got.shape[0] // 8):
        total = total + got[8 * n : 8 * n + 8, :]
    total = total[0:2] + total[2:4] + total[4:6] + total[6:8]
    live_total = total[0:1, 77:78]
    norm_value = norm[0]
    lane = iota((2, 128), 1)
    low = lane < 64
    wide = jnp.where((lane % 8 == 0) & (lane >= 64), total, 0.0)
    for step in (1, 2, 4):
        wide = wide + pltpu.roll(wide, step, 1)
    density = jnp.where(low, pltpu.roll(wide, 64, 1), total) / live_total
    ratio = density / norm_value + EPSILON
    bias = PREFACTOR * jnp.log(ratio)
    weight = jnp.exp(bias)
    force = -PREFACTOR * (total / live_total) / (norm_value * ratio)
    out = jnp.where(low, force, bias)
    results_out[...] = jnp.concatenate([out] * (got.shape[0] // 2), axis=0)
    place = lane % 8
    weight = jnp.where((lane >= 64) & (place >= 1) & (place <= 4), weight, 0.0)
    weight = pltpu.roll(weight[0:1], 63, 1)
    share = jnp.sum(jnp.where(lane == 69, density, 0.0)[0:1])
    share = jnp.where(lane[0:1] == 0, share, 0.0)
    packed = jnp.concatenate([rows[0:9], weight, share, rows[9:10], jnp.zeros((4, 128), F32)], axis=0)
    x = lax.axis_index("wx")
    merge_out[...] = pltpu.roll(packed, 64 * (x % 2) + 4 * (x // 2), 1)


def final_kernel(walker_count, got, results, centers, sigmas, heights, norm,
                 bias_out, force_out, heights_out, centers_out, sigmas_out, norm_out):
    half = results.shape[0] // 2
    turned = jnp.transpose(jnp.concatenate(
        [results[pl.ds(0, half, stride=2), :], results[pl.ds(1, half, stride=2), :]], axis=0
    ))
    for g in range(8):
        force_out[:, 128 * g : 128 * g + 128] = turned[8 * g : 8 * g + 8]
        bias_out[g : g + 1, :] = turned[64 + 8 * g : 65 + 8 * g]
    kernels = centers.shape[1]
    cand = jnp.concatenate([got[0] + got[2] + got[4] + got[6], got[1] + got[3] + got[5] + got[7]], axis=1)
    x = cand[0:8]
    slot = cand[8:9].astype(jnp.int32) - 1
    weight = cand[9:10]
    density_sum = jnp.sum(cand[10:11], axis=1, keepdims=True)
    placing = (iota((kernels, cand.shape[1]), 0) == slot).astype(BF16)
    c = centers[...]
    at = jnp.dot(jnp.concatenate(split3(c), axis=0).astype(BF16), placing, preferred_element_type=F32)
    offset = x - (at[0:8] + at[8:16] + at[16:24])
    sn = jnp.where(iota((8, 128), 0) == iota((8, 128), 1), got[0][11:12], 0.0)
    sn = jnp.sum(sn, axis=1, keepdims=True)
    feat = jnp.concatenate(
        [jnp.broadcast_to(weight, x.shape), weight * offset, weight * (offset * offset + sn * sn)], axis=0
    )
    sums = lax.dot_general(
        jnp.concatenate(split3(feat), axis=0).astype(BF16), placing, NT, preferred_element_type=F32
    )
    sums = sums[0:24] + sums[24:48] + sums[48:72]
    h = as_row(heights[...])
    new_h = h + sums[0:1]
    delta = sums[8:16] / new_h
    s = sigmas[...]
    centers_out[...] = c + delta
    sigmas_out[...] = jnp.sqrt((h * s * s + sums[16:24]) / new_h - delta * delta)
    heights_out[...] = jnp.concatenate(blocks(new_h), axis=0)
    norm_out[...] = jnp.log((1.0 - RATE) * norm[0] + RATE * density_sum / walker_count)


def call(kernel, outs, specs, scratch=(), limit=16 * 2**20):
    return pl.pallas_call(
        kernel,
        out_shape=outs,
        in_specs=specs,
        out_specs=[VMEM] * len(outs),
        scratch_shapes=list(scratch),
        compiler_params=pltpu.CompilerParams(vmem_limit_bytes=limit),
    )


def shape(*dims):
    return jax.ShapeDtypeStruct(dims, F32)


def per_device(walkers, centers, sigmas, heights, kernel_live, merge_target, new_sigma, norm_old):
    nk = lax.axis_size("kern")
    nw = lax.axis_size(WALK)
    kernels = centers.shape[1]
    count = walkers.shape[1]
    heights2 = heights.reshape(-1, 128)
    sums, rows = call(
        functools.partial(moments_kernel, nk),
        [shape(2 * nk, 128), shape(16, 128)],
        [HBM] * 7,
        [
            pltpu.VMEM((kernels, 128), BF16),
            pltpu.VMEM((48, kernels), BF16),
            pltpu.VMEM(walkers.shape, F32),
            pltpu.VMEM(centers.shape, F32),
            pltpu.VMEM(centers.shape, F32),
            pltpu.VMEM(heights2.shape, F32),
            pltpu.VMEM((count // 128, 128), jnp.int32),
            pltpu.SMEM(kernel_live.shape, jnp.int32),
            pltpu.SMEM(new_sigma.shape, F32),
            pltpu.SemaphoreType.DMA((7,)),
        ],
        limit=56 * 2**20,
    )(walkers, centers, sigmas, heights2, kernel_live, merge_target.reshape(-1, 128), new_sigma)
    sums = lax.all_to_all(sums.reshape(nk, 2, 128), "kern", 0, 0, tiled=True).reshape(2 * nk, 128)
    results, packed = call(
        results_kernel,
        [shape(2 * nk, 128), shape(16, 128)],
        [VMEM, VMEM, SMEM],
    )(sums, rows, norm_old)
    results = lax.all_to_all(results.reshape(nk, 2, 128), "kern", 0, 0, tiled=True).reshape(2 * nk, 128)
    packed = lax.all_gather(packed, "wc")
    packed = lax.all_gather(packed, "wx", axis_index_groups=NEAR)
    packed = lax.all_gather(packed, "wx", axis_index_groups=ACROSS).reshape(nw, 16, 128)
    bias, force, new_heights, new_centers, new_sigmas, log_norm = call(
        functools.partial(final_kernel, count * nw),
        [
            shape(count // 128, 128), shape(8, count), shape(*heights2.shape), shape(*centers.shape),
            shape(*centers.shape), shape(1, 1),
        ],
        [VMEM, VMEM, VMEM, VMEM, VMEM, SMEM],
    )(packed, results, centers, sigmas, heights2, norm_old)
    return (
        bias.reshape(-1), force, new_heights.reshape(-1), new_centers, new_sigmas, log_norm.reshape(-1)
    )


def solution(mesh):
    mesh = Mesh(mesh.devices.reshape(mesh.shape["kern"], -1, 2), ("kern", *WALK))
    in_specs = (
        P(None, WALK),
        P(None, "kern"),
        P(None, "kern"),
        P("kern"),
        P("kern"),
        P(WALK),
        P(),
        P(),
    )
    out_specs = (P(WALK), P(None, WALK), P("kern"), P(None, "kern"), P(None, "kern"), P())
    return jax.shard_map(
        per_device, mesh=mesh, in_specs=in_specs, out_specs=out_specs, check_vma=False
    )
```

```python
import functools
import jax
import jax.numpy as jnp
from jax import lax
from jax.experimental import pallas as pl
from jax.experimental.pallas import tpu as pltpu
from jax.sharding import Mesh
from jax.sharding import PartitionSpec as P

WALK = ("wx", "wc")
NEAR = [[0, 1], [2, 3]]
ACROSS = [[0, 3], [1, 2]]
PREFACTOR = 0.9
EPSILON = 0.01
RATE = 0.25
LOG2E = 1.4426950408889634
F32 = jnp.float32
BF16 = jnp.bfloat16
NT = (((1,), (1,)), ((), ()))
VMEM = pl.BlockSpec(memory_space=pltpu.VMEM)
SMEM = pl.BlockSpec(memory_space=pltpu.SMEM)
HBM = pl.BlockSpec(memory_space=pltpu.HBM)
BW = 128
BK = 256


def iota(dims, axis):
    return lax.broadcasted_iota(jnp.int32, dims, axis)


def split3(x):
    hi = x.astype(BF16).astype(F32)
    rest = x - hi
    mid = rest.astype(BF16).astype(F32)
    return (hi, mid, rest - mid)


def as_row(x):
    return jnp.concatenate([x[r : r + 1, :] for r in range(x.shape[0])], axis=1)


def blocks(x):
    return [x[:, 128 * g : 128 * g + 128] for g in range(x.shape[1] // 128)]


def moments_kernel(
    nk, walkers_in, centers_in, sigmas_in, heights_in, live_in, target_in, new_in,
    sums_out, rows_out,
    kt, mom, walkers, centers, sigmas, heights, target, live, new, sems,
):
    copies = [
        pltpu.make_async_copy(src, dst, sems.at[n])
        for n, (src, dst) in enumerate((
            (sigmas_in, sigmas), (centers_in, centers), (heights_in, heights), (walkers_in, walkers),
            (target_in, target), (live_in, live), (new_in, new),
        ))
    ]
    for copy in copies:
        copy.start()
    for copy in copies:
        copy.wait()
    kernels = centers.shape[1]
    count = walkers.shape[1]
    shard = lax.axis_index("kern")
    s = sigmas[...]
    c = centers[...]
    inv = 1.0 / (s * s)
    ca = c * inv
    const = as_row(jnp.log(heights[...])) - 0.5 * jnp.sum(c * ca, axis=0, keepdims=True)
    k1, k2, k3 = split3(jnp.concatenate([(-0.5 * LOG2E) * inv, LOG2E * ca], axis=0))
    c1, c2, c3 = split3(const * LOG2E)
    rows = jnp.concatenate(
        [k1, k2, k3, k1, k2, k1, c1, c2, c3, jnp.zeros((29, kernels), F32)], axis=0
    )
    for n, block in enumerate(blocks(rows)):
        kt[128 * n : 128 * n + 128, :] = jnp.transpose(block).astype(BF16)
    alive = (iota((1, kernels), 1) < live[0]).astype(F32)
    m1, m2, _ = split3(jnp.concatenate([inv, ca], axis=0) * alive)
    mom[...] = jnp.concatenate([m1, m2, alive, jnp.zeros((15, kernels), F32)], axis=0).astype(BF16)
    w = walkers[...]
    w1, w2, w3 = split3(jnp.concatenate([w * w, w], axis=0))
    ones = (iota((32, count), 0) < 3).astype(F32)
    feats = jnp.concatenate([w1, w1, w1, w2, w2, w3, ones], axis=0).astype(BF16)
    parts = []
    for i in range(count // BW):
        right = feats[:, BW * i : BW * i + BW]
        total = jnp.zeros((48, BW), F32)
        for j in range(kernels // BK):
            expo = jnp.dot(kt[BK * j : BK * j + BK], right, preferred_element_type=F32)
            e = jnp.exp2(expo)
            e1 = e.astype(BF16)
            e2 = (e - e1.astype(F32)).astype(BF16)
            m = mom[:, BK * j : BK * j + BK]
            total += jnp.dot(m, e1, preferred_element_type=F32)
            total += jnp.dot(m, e2, preferred_element_type=F32)
        parts.append(total)
    summed = jnp.concatenate(parts, axis=1)
    density = summed[32:33]
    slope = (summed[8:16] + summed[24:32]) - w * (summed[0:8] + summed[16:24])
    t = as_row(target[...])
    shard_of = t // kernels
    slot_of = t - shard_of * kernels
    member = (iota((nk, count), 0) == shard_of).astype(F32)
    member16 = member.astype(BF16)
    ra = iota((128, 256), 0)
    rb = iota((128, 256), 1)
    before = ((ra < rb) | (rb >= 128)).astype(BF16)
    counts = jnp.dot(jnp.concatenate(blocks(member16), axis=0), before, preferred_element_type=F32)
    base = jnp.zeros((nk, 128), F32)
    ranks = []
    for n, block in enumerate(blocks(member)):
        here = counts[nk * n : nk * n + nk]
        ranks.append(jnp.sum(block * (base + here[:, 0:128]), axis=0, keepdims=True))
        base = base + here[:, 128:256]
    rank = jnp.concatenate(ranks, axis=1).astype(jnp.int32)
    lane_of = 8 * (rank % 8) + rank // 8
    placed = (iota((64, count), 0) == lane_of + 1).astype(F32)
    d1, d2, d3 = split3(density)
    terms = jnp.concatenate([placed * d3, placed * d1, placed * d2, jnp.zeros((64, count), F32)], axis=0)
    compact = lax.dot_general(member16, terms.astype(BF16), NT, preferred_element_type=F32)
    near = compact[:, 0:128]
    compact = near + pltpu.roll(near, 64, 1) + pltpu.roll(compact[:, 128:256], 64, 1)
    lane = iota((nk, 128), 1)
    compact = jnp.where(lane < 64, 0.0, compact)
    compact = jnp.where(lane == 69, jnp.sum(density), compact)
    compact = jnp.where(lane == 77, live[0].astype(F32), compact)
    first = (iota((8, 1), 0) == 0).astype(F32)
    turned = jnp.transpose(jnp.concatenate(blocks(slope) + blocks(density * first), axis=0))
    sums_out[pl.ds(0, nk, stride=2), :] = turned[0:nk] + compact
    sums_out[pl.ds(1, nk, stride=2), :] = turned[nk : 2 * nk]
    mine = (iota((64, count), 0) == lane_of) & (shard_of == shard)
    mine = jnp.concatenate([mine.astype(F32), jnp.zeros((64, count), F32)], axis=0).astype(BF16)
    x = jnp.concatenate([w, jnp.broadcast_to((slot_of + 1).astype(F32), (8, count))], axis=0)
    picked = lax.dot_general(
        jnp.concatenate(split3(x), axis=0).astype(BF16), mine, NT, preferred_element_type=F32
    )
    lane = iota((1, 128), 1)
    widths = jnp.zeros((1, 128), F32)
    for d in range(8):
        widths = jnp.where(lane == d, new[d], widths)
    picked = picked[0:9] + picked[16:25] + picked[32:41]
    rows_out[...] = jnp.concatenate([picked, widths, jnp.zeros((6, 128), F32)], axis=0)


def results_kernel(got, rows, norm, results_out, merge_out):
    total = got[0:8, :]
    for n in range(1, got.shape[0] // 8):
        total = total + got[8 * n : 8 * n + 8, :]
    total = total[0:2] + total[2:4] + total[4:6] + total[6:8]
    live_total = total[0:1, 77:78]
    norm_value = norm[0]
    lane = iota((2, 128), 1)
    low = lane < 64
    wide = jnp.where((lane % 8 == 0) & (lane >= 64), total, 0.0)
    for step in (1, 2, 4):
        wide = wide + pltpu.roll(wide, step, 1)
    density = jnp.where(low, pltpu.roll(wide, 64, 1), total) / live_total
    ratio = density / norm_value + EPSILON
    bias = PREFACTOR * jnp.log(ratio)
    weight = jnp.exp(bias)
    force = -PREFACTOR * (total / live_total) / (norm_value * ratio)
    out = jnp.where(low, force, bias)
    results_out[...] = jnp.concatenate([out] * (got.shape[0] // 2), axis=0)
    place = lane % 8
    weight = jnp.where((lane >= 64) & (place >= 1) & (place <= 4), weight, 0.0)
    weight = pltpu.roll(weight[0:1], 63, 1)
    share = jnp.sum(jnp.where(lane == 69, density, 0.0)[0:1])
    share = jnp.where(lane[0:1] == 0, share, 0.0)
    packed = jnp.concatenate([rows[0:9], weight, share, rows[9:10], jnp.zeros((4, 128), F32)], axis=0)
    x = lax.axis_index("wx")
    merge_out[...] = pltpu.roll(packed, 64 * (x % 2) + 4 * (x // 2), 1)


def final_kernel(walker_count, got, results, centers, sigmas, heights, norm,
                 bias_out, force_out, heights_out, centers_out, sigmas_out, norm_out):
    half = results.shape[0] // 2
    turned = jnp.transpose(jnp.concatenate(
        [results[pl.ds(0, half, stride=2), :], results[pl.ds(1, half, stride=2), :]], axis=0
    ))
    for g in range(8):
        force_out[:, 128 * g : 128 * g + 128] = turned[8 * g : 8 * g + 8]
        bias_out[g : g + 1, :] = turned[64 + 8 * g : 65 + 8 * g]
    kernels = centers.shape[1]
    cand = jnp.concatenate([got[0] + got[2] + got[4] + got[6], got[1] + got[3] + got[5] + got[7]], axis=1)
    x = cand[0:8]
    slot = cand[8:9].astype(jnp.int32) - 1
    weight = cand[9:10]
    density_sum = jnp.sum(cand[10:11], axis=1, keepdims=True)
    placing = (iota((kernels, cand.shape[1]), 0) == slot).astype(BF16)
    c = centers[...]
    at = jnp.dot(jnp.concatenate(split3(c), axis=0).astype(BF16), placing, preferred_element_type=F32)
    offset = x - (at[0:8] + at[8:16] + at[16:24])
    sn = jnp.where(iota((8, 128), 0) == iota((8, 128), 1), got[0][11:12], 0.0)
    sn = jnp.sum(sn, axis=1, keepdims=True)
    feat = jnp.concatenate(
        [jnp.broadcast_to(weight, x.shape), weight * offset, weight * (offset * offset + sn * sn)], axis=0
    )
    sums = lax.dot_general(
        jnp.concatenate(split3(feat), axis=0).astype(BF16), placing, NT, preferred_element_type=F32
    )
    sums = sums[0:24] + sums[24:48] + sums[48:72]
    h = as_row(heights[...])
    new_h = h + sums[0:1]
    delta = sums[8:16] / new_h
    s = sigmas[...]
    centers_out[...] = c + delta
    sigmas_out[...] = jnp.sqrt((h * s * s + sums[16:24]) / new_h - delta * delta)
    heights_out[...] = jnp.concatenate(blocks(new_h), axis=0)
    norm_out[...] = jnp.log((1.0 - RATE) * norm[0] + RATE * density_sum / walker_count)


def call(kernel, outs, specs, scratch=(), limit=16 * 2**20):
    return pl.pallas_call(
        kernel,
        out_shape=outs,
        in_specs=specs,
        out_specs=[VMEM] * len(outs),
        scratch_shapes=list(scratch),
        compiler_params=pltpu.CompilerParams(vmem_limit_bytes=limit),
    )


def shape(*dims):
    return jax.ShapeDtypeStruct(dims, F32)


def per_device(walkers, centers, sigmas, heights, kernel_live, merge_target, new_sigma, norm_old):
    nk = lax.axis_size("kern")
    nw = lax.axis_size(WALK)
    kernels = centers.shape[1]
    count = walkers.shape[1]
    heights2 = heights.reshape(-1, 128)
    sums, rows = call(
        functools.partial(moments_kernel, nk),
        [shape(2 * nk, 128), shape(16, 128)],
        [HBM] * 7,
        [
            pltpu.VMEM((kernels, 128), BF16),
            pltpu.VMEM((48, kernels), BF16),
            pltpu.VMEM(walkers.shape, F32),
            pltpu.VMEM(centers.shape, F32),
            pltpu.VMEM(centers.shape, F32),
            pltpu.VMEM(heights2.shape, F32),
            pltpu.VMEM((count // 128, 128), jnp.int32),
            pltpu.SMEM(kernel_live.shape, jnp.int32),
            pltpu.SMEM(new_sigma.shape, F32),
            pltpu.SemaphoreType.DMA((7,)),
        ],
        limit=56 * 2**20,
    )(walkers, centers, sigmas, heights2, kernel_live, merge_target.reshape(-1, 128), new_sigma)
    sums = lax.all_to_all(sums.reshape(nk, 2, 128), "kern", 0, 0, tiled=True).reshape(2 * nk, 128)
    results, packed = call(
        results_kernel,
        [shape(2 * nk, 128), shape(16, 128)],
        [VMEM, VMEM, SMEM],
    )(sums, rows, norm_old)
    results = lax.all_to_all(results.reshape(nk, 2, 128), "kern", 0, 0, tiled=True).reshape(2 * nk, 128)
    packed = lax.all_gather(packed, "wc")
    packed = lax.all_gather(packed, "wx", axis_index_groups=NEAR)
    packed = lax.all_gather(packed, "wx", axis_index_groups=ACROSS).reshape(nw, 16, 128)
    bias, force, new_heights, new_centers, new_sigmas, log_norm = call(
        functools.partial(final_kernel, count * nw),
        [
            shape(count // 128, 128), shape(8, count), shape(*heights2.shape), shape(*centers.shape),
            shape(*centers.shape), shape(1, 1),
        ],
        [VMEM, VMEM, VMEM, VMEM, VMEM, SMEM],
    )(packed, results, centers, sigmas, heights2, norm_old)
    return (
        bias.reshape(-1), force, new_heights.reshape(-1), new_centers, new_sigmas, log_norm.reshape(-1)
    )


def solution(mesh):
    mesh = Mesh(mesh.devices.reshape(mesh.shape["kern"], -1, 2), ("kern", *WALK))
    in_specs = (
        P(None, WALK),
        P(None, "kern"),
        P(None, "kern"),
        P("kern"),
        P("kern"),
        P(WALK),
        P(),
        P(),
    )
    out_specs = (P(WALK), P(None, WALK), P("kern"), P(None, "kern"), P(None, "kern"), P())
    return jax.shard_map(
        per_device, mesh=mesh, in_specs=in_specs, out_specs=out_specs, check_vma=False
    )
```

```python
import functools
import jax
import jax.numpy as jnp
from jax import lax
from jax.experimental import pallas as pl
from jax.experimental.pallas import tpu as pltpu
from jax.sharding import Mesh
from jax.sharding import PartitionSpec as P

WALK = ("wx", "wc")
NEAR = [[0, 1], [2, 3]]
ACROSS = [[0, 3], [1, 2]]
PREFACTOR = 0.9
EPSILON = 0.01
RATE = 0.25
LOG2E = 1.4426950408889634
F32 = jnp.float32
BF16 = jnp.bfloat16
NT = (((1,), (1,)), ((), ()))
VMEM = pl.BlockSpec(memory_space=pltpu.VMEM)
SMEM = pl.BlockSpec(memory_space=pltpu.SMEM)
HBM = pl.BlockSpec(memory_space=pltpu.HBM)
BW = 128
BK = 128


def iota(dims, axis):
    return lax.broadcasted_iota(jnp.int32, dims, axis)


def split3(x):
    hi = x.astype(BF16).astype(F32)
    rest = x - hi
    mid = rest.astype(BF16).astype(F32)
    return (hi, mid, rest - mid)


def as_row(x):
    return jnp.concatenate([x[r : r + 1, :] for r in range(x.shape[0])], axis=1)


def blocks(x):
    return [x[:, 128 * g : 128 * g + 128] for g in range(x.shape[1] // 128)]


def moments_kernel(
    nk, walkers_in, centers_in, sigmas_in, heights_in, live_in, target_in, new_in,
    sums_out, rows_out,
    kt, mom, walkers, centers, sigmas, heights, target, live, new, sems,
):
    copies = [
        pltpu.make_async_copy(src, dst, sems.at[n])
        for n, (src, dst) in enumerate((
            (sigmas_in, sigmas), (centers_in, centers), (heights_in, heights), (walkers_in, walkers),
            (target_in, target), (live_in, live), (new_in, new),
        ))
    ]
    for copy in copies:
        copy.start()
    for copy in copies:
        copy.wait()
    kernels = centers.shape[1]
    count = walkers.shape[1]
    shard = lax.axis_index("kern")
    s = sigmas[...]
    c = centers[...]
    inv = 1.0 / (s * s)
    ca = c * inv
    const = as_row(jnp.log(heights[...])) - 0.5 * jnp.sum(c * ca, axis=0, keepdims=True)
    k1, k2, k3 = split3(jnp.concatenate([(-0.5 * LOG2E) * inv, LOG2E * ca], axis=0))
    c1, c2, c3 = split3(const * LOG2E)
    rows = jnp.concatenate(
        [k1, k2, k3, k1, k2, k1, c1, c2, c3, jnp.zeros((29, kernels), F32)], axis=0
    )
    for n, block in enumerate(blocks(rows)):
        kt[128 * n : 128 * n + 128, :] = jnp.transpose(block).astype(BF16)
    alive = (iota((1, kernels), 1) < live[0]).astype(F32)
    m1, m2, _ = split3(jnp.concatenate([inv, ca], axis=0) * alive)
    mom[...] = jnp.concatenate([m1, m2, alive, jnp.zeros((15, kernels), F32)], axis=0).astype(BF16)
    w = walkers[...]
    w1, w2, w3 = split3(jnp.concatenate([w * w, w], axis=0))
    ones = (iota((32, count), 0) < 3).astype(F32)
    feats = jnp.concatenate([w1, w1, w1, w2, w2, w3, ones], axis=0).astype(BF16)
    parts = []
    for i in range(count // BW):
        right = feats[:, BW * i : BW * i + BW]
        total = jnp.zeros((48, BW), F32)
        for j in range(kernels // BK):
            expo = jnp.dot(kt[BK * j : BK * j + BK], right, preferred_element_type=F32)
            e = jnp.exp2(expo)
            e1 = e.astype(BF16)
            e2 = (e - e1.astype(F32)).astype(BF16)
            m = mom[:, BK * j : BK * j + BK]
            total += jnp.dot(m, e1, preferred_element_type=F32)
            total += jnp.dot(m, e2, preferred_element_type=F32)
        parts.append(total)
    summed = jnp.concatenate(parts, axis=1)
    density = summed[32:33]
    slope = (summed[8:16] + summed[24:32]) - w * (summed[0:8] + summed[16:24])
    t = as_row(target[...])
    shard_of = t // kernels
    slot_of = t - shard_of * kernels
    member = (iota((nk, count), 0) == shard_of).astype(F32)
    member16 = member.astype(BF16)
    ra = iota((128, 256), 0)
    rb = iota((128, 256), 1)
    before = ((ra < rb) | (rb >= 128)).astype(BF16)
    counts = jnp.dot(jnp.concatenate(blocks(member16), axis=0), before, preferred_element_type=F32)
    base = jnp.zeros((nk, 128), F32)
    ranks = []
    for n, block in enumerate(blocks(member)):
        here = counts[nk * n : nk * n + nk]
        ranks.append(jnp.sum(block * (base + here[:, 0:128]), axis=0, keepdims=True))
        base = base + here[:, 128:256]
    rank = jnp.concatenate(ranks, axis=1).astype(jnp.int32)
    lane_of = 8 * (rank % 8) + rank // 8
    placed = (iota((64, count), 0) == lane_of + 1).astype(F32)
    d1, d2, d3 = split3(density)
    terms = jnp.concatenate([placed * d3, placed * d1, placed * d2, jnp.zeros((64, count), F32)], axis=0)
    compact = lax.dot_general(member16, terms.astype(BF16), NT, preferred_element_type=F32)
    near = compact[:, 0:128]
    compact = near + pltpu.roll(near, 64, 1) + pltpu.roll(compact[:, 128:256], 64, 1)
    lane = iota((nk, 128), 1)
    compact = jnp.where(lane < 64, 0.0, compact)
    compact = jnp.where(lane == 69, jnp.sum(density), compact)
    compact = jnp.where(lane == 77, live[0].astype(F32), compact)
    first = (iota((8, 1), 0) == 0).astype(F32)
    turned = jnp.transpose(jnp.concatenate(blocks(slope) + blocks(density * first), axis=0))
    sums_out[pl.ds(0, nk, stride=2), :] = turned[0:nk] + compact
    sums_out[pl.ds(1, nk, stride=2), :] = turned[nk : 2 * nk]
    mine = (iota((64, count), 0) == lane_of) & (shard_of == shard)
    mine = jnp.concatenate([mine.astype(F32), jnp.zeros((64, count), F32)], axis=0).astype(BF16)
    x = jnp.concatenate([w, jnp.broadcast_to((slot_of + 1).astype(F32), (8, count))], axis=0)
    picked = lax.dot_general(
        jnp.concatenate(split3(x), axis=0).astype(BF16), mine, NT, preferred_element_type=F32
    )
    lane = iota((1, 128), 1)
    widths = jnp.zeros((1, 128), F32)
    for d in range(8):
        widths = jnp.where(lane == d, new[d], widths)
    picked = picked[0:9] + picked[16:25] + picked[32:41]
    rows_out[...] = jnp.concatenate([picked, widths, jnp.zeros((6, 128), F32)], axis=0)


def results_kernel(got, rows, norm, results_out, merge_out):
    total = got[0:8, :]
    for n in range(1, got.shape[0] // 8):
        total = total + got[8 * n : 8 * n + 8, :]
    total = total[0:2] + total[2:4] + total[4:6] + total[6:8]
    live_total = total[0:1, 77:78]
    norm_value = norm[0]
    lane = iota((2, 128), 1)
    low = lane < 64
    wide = jnp.where((lane % 8 == 0) & (lane >= 64), total, 0.0)
    for step in (1, 2, 4):
        wide = wide + pltpu.roll(wide, step, 1)
    density = jnp.where(low, pltpu.roll(wide, 64, 1), total) / live_total
    ratio = density / norm_value + EPSILON
    bias = PREFACTOR * jnp.log(ratio)
    weight = jnp.exp(bias)
    force = -PREFACTOR * (total / live_total) / (norm_value * ratio)
    out = jnp.where(low, force, bias)
    results_out[...] = jnp.concatenate([out] * (got.shape[0] // 2), axis=0)
    place = lane % 8
    weight = jnp.where((lane >= 64) & (place >= 1) & (place <= 4), weight, 0.0)
    weight = pltpu.roll(weight[0:1], 63, 1)
    share = jnp.sum(jnp.where(lane == 69, density, 0.0)[0:1])
    share = jnp.where(lane[0:1] == 0, share, 0.0)
    packed = jnp.concatenate([rows[0:9], weight, share, rows[9:10], jnp.zeros((4, 128), F32)], axis=0)
    x = lax.axis_index("wx")
    merge_out[...] = pltpu.roll(packed, 64 * (x % 2) + 4 * (x // 2), 1)


def final_kernel(walker_count, got, results, centers, sigmas, heights, norm,
                 bias_out, force_out, heights_out, centers_out, sigmas_out, norm_out):
    half = results.shape[0] // 2
    turned = jnp.transpose(jnp.concatenate(
        [results[pl.ds(0, half, stride=2), :], results[pl.ds(1, half, stride=2), :]], axis=0
    ))
    for g in range(8):
        force_out[:, 128 * g : 128 * g + 128] = turned[8 * g : 8 * g + 8]
        bias_out[g : g + 1, :] = turned[64 + 8 * g : 65 + 8 * g]
    kernels = centers.shape[1]
    cand = jnp.concatenate([got[0] + got[2] + got[4] + got[6], got[1] + got[3] + got[5] + got[7]], axis=1)
    x = cand[0:8]
    slot = cand[8:9].astype(jnp.int32) - 1
    weight = cand[9:10]
    density_sum = jnp.sum(cand[10:11], axis=1, keepdims=True)
    placing = (iota((kernels, cand.shape[1]), 0) == slot).astype(BF16)
    c = centers[...]
    at = jnp.dot(jnp.concatenate(split3(c), axis=0).astype(BF16), placing, preferred_element_type=F32)
    offset = x - (at[0:8] + at[8:16] + at[16:24])
    sn = jnp.where(iota((8, 128), 0) == iota((8, 128), 1), got[0][11:12], 0.0)
    sn = jnp.sum(sn, axis=1, keepdims=True)
    feat = jnp.concatenate(
        [jnp.broadcast_to(weight, x.shape), weight * offset, weight * (offset * offset + sn * sn)], axis=0
    )
    sums = lax.dot_general(
        jnp.concatenate(split3(feat), axis=0).astype(BF16), placing, NT, preferred_element_type=F32
    )
    sums = sums[0:24] + sums[24:48] + sums[48:72]
    h = as_row(heights[...])
    new_h = h + sums[0:1]
    delta = sums[8:16] / new_h
    s = sigmas[...]
    centers_out[...] = c + delta
    sigmas_out[...] = jnp.sqrt((h * s * s + sums[16:24]) / new_h - delta * delta)
    heights_out[...] = jnp.concatenate(blocks(new_h), axis=0)
    norm_out[...] = jnp.log((1.0 - RATE) * norm[0] + RATE * density_sum / walker_count)


def call(kernel, outs, specs, scratch=(), limit=16 * 2**20):
    return pl.pallas_call(
        kernel,
        out_shape=outs,
        in_specs=specs,
        out_specs=[VMEM] * len(outs),
        scratch_shapes=list(scratch),
        compiler_params=pltpu.CompilerParams(vmem_limit_bytes=limit),
    )


def shape(*dims):
    return jax.ShapeDtypeStruct(dims, F32)


def per_device(walkers, centers, sigmas, heights, kernel_live, merge_target, new_sigma, norm_old):
    nk = lax.axis_size("kern")
    nw = lax.axis_size(WALK)
    kernels = centers.shape[1]
    count = walkers.shape[1]
    heights2 = heights.reshape(-1, 128)
    sums, rows = call(
        functools.partial(moments_kernel, nk),
        [shape(2 * nk, 128), shape(16, 128)],
        [HBM] * 7,
        [
            pltpu.VMEM((kernels, 128), BF16),
            pltpu.VMEM((48, kernels), BF16),
            pltpu.VMEM(walkers.shape, F32),
            pltpu.VMEM(centers.shape, F32),
            pltpu.VMEM(centers.shape, F32),
            pltpu.VMEM(heights2.shape, F32),
            pltpu.VMEM((count // 128, 128), jnp.int32),
            pltpu.SMEM(kernel_live.shape, jnp.int32),
            pltpu.SMEM(new_sigma.shape, F32),
            pltpu.SemaphoreType.DMA((7,)),
        ],
        limit=56 * 2**20,
    )(walkers, centers, sigmas, heights2, kernel_live, merge_target.reshape(-1, 128), new_sigma)
    sums = lax.all_to_all(sums.reshape(nk, 2, 128), "kern", 0, 0, tiled=True).reshape(2 * nk, 128)
    results, packed = call(
        results_kernel,
        [shape(2 * nk, 128), shape(16, 128)],
        [VMEM, VMEM, SMEM],
    )(sums, rows, norm_old)
    results = lax.all_to_all(results.reshape(nk, 2, 128), "kern", 0, 0, tiled=True).reshape(2 * nk, 128)
    packed = lax.all_gather(packed, "wc")
    packed = lax.all_gather(packed, "wx", axis_index_groups=NEAR)
    packed = lax.all_gather(packed, "wx", axis_index_groups=ACROSS).reshape(nw, 16, 128)
    bias, force, new_heights, new_centers, new_sigmas, log_norm = call(
        functools.partial(final_kernel, count * nw),
        [
            shape(count // 128, 128), shape(8, count), shape(*heights2.shape), shape(*centers.shape),
            shape(*centers.shape), shape(1, 1),
        ],
        [VMEM, VMEM, VMEM, VMEM, VMEM, SMEM],
    )(packed, results, centers, sigmas, heights2, norm_old)
    return (
        bias.reshape(-1), force, new_heights.reshape(-1), new_centers, new_sigmas, log_norm.reshape(-1)
    )


def solution(mesh):
    mesh = Mesh(mesh.devices.reshape(mesh.shape["kern"], -1, 2), ("kern", *WALK))
    in_specs = (
        P(None, WALK),
        P(None, "kern"),
        P(None, "kern"),
        P("kern"),
        P("kern"),
        P(WALK),
        P(),
        P(),
    )
    out_specs = (P(WALK), P(None, WALK), P("kern"), P(None, "kern"), P(None, "kern"), P())
    return jax.shard_map(
        per_device, mesh=mesh, in_specs=in_specs, out_specs=out_specs, check_vma=False
    )
```
